32 devices in a mesh: view: 8 (over y, x, core), tile: 4 (over z).
Axes of the slice: x: 2, y: 2, z: 4, core: 2. Of those that a mesh axis runs over, the one named last changes fastest.
Arguments:
- centers: bfloat16 [96, 2, 128], P('tile'), may hold values from 4 to 28
- log_scales: bfloat16 [96, 2, 128], P('tile'), may hold values from -4 to -1.5
- correlation: bfloat16 [96, 128], P('tile'), may hold values from -0.59765625 to 0.59765625
- opacity_logit: bfloat16 [96, 128], P('tile'), may hold values from -6.5 to -2
- features: bfloat16 [96, 128, 128], P('tile'), may hold values from -16 to 16
- view_offset: float32 [8, 2], P('view'), may hold values from -3 to 3
- block_list: int32 [8, 8, 8], P('view', 'tile'), may hold values from 0 to 95, as said below
- pad_count: int32 [8, 8], P('view', 'tile'), may hold values from 0 to 7, as said below
- block_home: int32 [96], replicated, may hold values from 0 to 95, as said below
- image_grad: bfloat16 [8, 8, 1024, 128], P('view', 'tile'), may hold values from -6 to 6
Outputs:
- image: bfloat16 [8, 8, 1024, 128], P('view', 'tile')
- grad_centers: float32 [96, 2, 128], P('tile')
- grad_log_scales: float32 [96, 2, 128], P('tile')
- grad_correlation: float32 [96, 128], P('tile')
- grad_opacity: float32 [96, 128], P('tile')
- grad_features: float32 [96, 128, 128], P('tile')
The draws below stay inside these ranges and needn't reach their ends.
Inputs may be any that keep to these rules, and one draw needn't show every extreme that they name: `block_list`: the 2 lists of one view on one index of tile name at most 5 entries whose blocks lie in one shard of 24 rows (through block_home), padded entries included; in every such list set some shard is named exactly 5 times. Padded entries hold valid ids. `pad_count`: the first tile of every view has no padding. `block_home`: A permutation of the block ids.
All inputs are finite; a program needn't handle non-finite values.
Results may differ from the reference program's by a relative error of at most 0.0055.
Values may be sent and summed in bfloat16 or wider, within the bound.
A program may use at most 64 MiB of HBM per device.

```python
import jax
import jax.numpy as jnp
from jax import lax

F = 128
BLOCK = 128
TILE_W = 32
MAXB = 8
TILES_DEV = 2
BLK_DEV = 24
VIEWS = 8
TILES = 8
NBLK_ALL = 96
PIX = 1024
CAP = 5
N_TILE = 4


def layout_tables(key):
    base_key = jax.random.fold_in(key, 7)
    home_key, owner_key, order_key, start_key, padding_key = jax.random.split(base_key, 5)
    home_table = jax.random.permutation(home_key, NBLK_ALL).astype(jnp.int32)
    inverse_table = jnp.argsort(home_table, stable=True).astype(jnp.int32)
    device_count = VIEWS * N_TILE
    slot_count = TILES_DEV * MAXB
    owner_perms = jax.vmap(lambda one_key: jax.random.permutation(one_key, N_TILE))(jax.random.split(owner_key, device_count)).astype(jnp.int32)
    slot_order = jax.vmap(lambda one_key: jax.random.permutation(one_key, slot_count))(jax.random.split(order_key, device_count)).astype(jnp.int32)
    owner_of = jnp.take_along_axis(owner_perms, slot_order // CAP, axis=1)
    starts = jax.random.randint(start_key, (device_count, N_TILE), 0, BLK_DEV).astype(jnp.int32)
    local_slot = (jnp.take_along_axis(starts, owner_of, axis=1) + slot_order % CAP) % BLK_DEV
    storage = owner_of * BLK_DEV + local_slot
    block_ids = jnp.take(inverse_table, storage.reshape(-1)).reshape(VIEWS, TILES, MAXB).astype(jnp.int32)
    padding = jax.random.randint(padding_key, (VIEWS, TILES), 0, MAXB).astype(jnp.int32)
    padding = padding.at[:, 0].set(0)
    return (home_table, block_ids, padding)


def draw_block_list(key, part):
    return layout_tables(key)[1]


def draw_pad_count(key, part):
    return layout_tables(key)[2]


def draw_block_home(key, part):
    return layout_tables(key)[0]


def block_levels(rng, dims, pieces, smallest, top_value):
    gain = 1.0
    for axis_at, shards_of in pieces:
        draws = jax.random.uniform(jax.random.fold_in(jax.random.fold_in(rng, 6), axis_at), (shards_of,), jnp.float32, smallest / len(pieces), top_value / len(pieces))
        gain = gain * jnp.repeat(jnp.exp(draws), dims[axis_at] // shards_of).reshape((-1,) + (1,) * (len(dims) - 1 - axis_at))
    return gain


def gaussian(own_key, shape, width, limit, shards=(), kind=jnp.bfloat16):
    array = width * jax.random.normal(own_key, shape, jnp.float32)
    if shards:
        array = array * block_levels(own_key, shape, shards, -0.22, 0.18)
    return jnp.clip(array, -limit, limit).astype(kind)


def setup_inputs(seed: int = 0) -> dict:
    keys = jax.random.split(jax.random.key(seed), 11)
    return {
        "centers": jnp.clip(4.0 + 24.0 * jax.random.uniform(keys[0], (NBLK_ALL, 2, BLOCK), jnp.float32) ** block_levels(keys[0], (NBLK_ALL, 2, BLOCK), ((0, 4),), -0.2, 0.2), 4.0, 28.0).astype(jnp.bfloat16),
        "log_scales": jnp.clip(-4.0 + 2.5 * jax.random.uniform(keys[1], (NBLK_ALL, 2, BLOCK), jnp.float32) ** block_levels(keys[1], (NBLK_ALL, 2, BLOCK), ((0, 4),), -0.2, 0.2), -4.0, -1.5).astype(jnp.bfloat16),
        "correlation": jnp.clip(jax.random.uniform(keys[2], (NBLK_ALL, BLOCK), jnp.float32, -0.59765625, 0.59765625) * block_levels(keys[2], (NBLK_ALL, BLOCK), ((0, 4),), -0.4, 0.0), -0.59765625, 0.59765625).astype(jnp.bfloat16),
        "opacity_logit": jnp.clip(-6.5 + 4.5 * jax.random.uniform(keys[3], (NBLK_ALL, BLOCK), jnp.float32) ** block_levels(keys[3], (NBLK_ALL, BLOCK), ((0, 4),), -0.2, 0.2), -6.5, -2.0).astype(jnp.bfloat16),
        "features": gaussian(keys[4], (NBLK_ALL, BLOCK, F), 4.0, 16.0, ((0, 4),)),
        "view_offset": jnp.clip(jax.random.uniform(keys[5], (VIEWS, 2), jnp.float32, -3.0, 3.0) * block_levels(keys[5], (VIEWS, 2), ((0, 8),), -0.4, 0.0), -3.0, 3.0),
        "block_list": draw_block_list(jax.random.fold_in(keys[10], 71), 0),
        "pad_count": draw_pad_count(jax.random.fold_in(keys[10], 71), 0),
        "block_home": draw_block_home(jax.random.fold_in(keys[10], 71), 0),
        "image_grad": gaussian(keys[9], (VIEWS, TILES, PIX, F), 1.0, 6.0, ((0, 8), (1, 4))),
    }


def pixel_grid():
    pixel_index = jnp.arange(TILE_W * TILE_W, dtype=jnp.int32)
    across = (pixel_index % TILE_W).astype(jnp.float32) + 0.5
    downward = (pixel_index // TILE_W).astype(jnp.float32) + 0.5
    return (across, downward)

def render_tile(tensors, alive_mask, offset):
    across, downward = pixel_grid()
    feature_width = tensors[4].shape[-1]

    def block_step(running, block_data):
        log_trans, colors = running
        center, log_scale, correl, opacity, feature, alive_flag = block_data
        delta_x = across[:, None] - (center[0] + offset[0])[None, :]
        delta_y = downward[:, None] - (center[1] + offset[1])[None, :]
        coef_a = jnp.exp(log_scale[0])
        coef_c = jnp.exp(log_scale[1])
        coef_b = correl * jnp.sqrt(coef_a * coef_c)
        quadric = coef_a[None, :] * delta_x * delta_x + 2.0 * coef_b[None, :] * delta_x * delta_y + coef_c[None, :] * delta_y * delta_y
        alphas = jax.nn.sigmoid(opacity)[None, :] * jnp.exp(-0.5 * quadric) * alive_flag
        log_keep = jnp.log1p(-alphas)
        before = jnp.cumsum(log_keep, axis=1) - log_keep
        weight = (alphas * jnp.exp(log_trans[:, None] + before)).astype(jnp.bfloat16)
        colors = colors + jnp.dot(weight, feature.astype(jnp.bfloat16), preferred_element_type=jnp.float32)
        log_trans = log_trans + lax.optimization_barrier(jnp.sum(log_keep, axis=1))
        return ((log_trans, colors), None)
    start_state = (jnp.zeros((across.shape[0],), jnp.float32), jnp.zeros((across.shape[0], feature_width), jnp.float32))
    (log_trans, colors), unused = lax.scan(jax.checkpoint(block_step), start_state, tuple(tensors) + (alive_mask,))
    return colors

def reference(centers, log_scales, correlation, opacity_logit, features, view_offset, block_list, pad_count, block_home, image_grad):
    flat_lists = block_list.reshape(VIEWS * TILES, MAXB)
    flat_pads = pad_count.reshape(VIEWS * TILES)
    flat_grad = image_grad.reshape(VIEWS * TILES, PIX, F)
    view_of = jnp.arange(VIEWS * TILES, dtype=jnp.int32) // TILES
    params = (centers, log_scales, correlation, opacity_logit, features)
    zero_sums = tuple((jnp.zeros(array_in.shape, jnp.float32) for array_in in params))

    def per_tile(totals, item_data):
        block_ids, pad_here, cotangent, view_index = item_data
        tile_rows = jnp.take(block_home, block_ids).astype(jnp.int32)
        inputs = tuple((jnp.take(array_in, tile_rows, axis=0).astype(jnp.float32) for array_in in params))
        alive_mask = (jnp.arange(MAXB, dtype=jnp.int32) < MAXB - pad_here).astype(jnp.float32)
        offset = view_offset[view_index]
        colors, pullback = jax.vjp(lambda *tensors: render_tile(tensors, alive_mask, offset), *inputs)
        grad_set = pullback(cotangent.astype(jnp.float32))
        totals = tuple((total_in.at[tile_rows].add(grad_in.astype(jnp.float32)) for total_in, grad_in in zip(totals, grad_set)))
        return (totals, colors.astype(jnp.bfloat16))
    totals, images = lax.scan(per_tile, zero_sums, (flat_lists, flat_pads, flat_grad, view_of))
    return (images.reshape(VIEWS, TILES, PIX, F), totals[0], totals[1], totals[2], totals[3], totals[4])
```

```python
import functools

import jax
import jax.numpy as jnp
from jax import lax
from jax.experimental import pallas as pl
from jax.experimental.pallas import tpu as pltpu
from jax.sharding import PartitionSpec as P

TILE_W = 32
ROWS = 16
LOG2E = 1.4426950408889634
SMEM = pl.BlockSpec(memory_space=pltpu.SMEM)
VMEM = pl.BlockSpec(memory_space=pltpu.VMEM)
ANY = pl.BlockSpec(memory_space=pl.ANY)
MESH = pl.DeviceIdType.MESH


def f32dot(a, b):
    return jnp.dot(a, b, preferred_element_type=jnp.float32)


def transposed(a):
    return a.astype(jnp.float32).T.astype(a.dtype)


def basis_of(pixel, kind):
    half = TILE_W // 2
    k = pixel % TILE_W - half
    j = pixel // TILE_W - half
    out = jnp.where(kind == 0, 1, 0)
    out = jnp.where(kind == 1, k, out)
    out = jnp.where(kind == 2, j, out)
    out = jnp.where(kind == 3, k * k, out)
    out = jnp.where(kind == 4, k * j, out)
    out = jnp.where(kind == 5, j * j, out)
    return out.astype(jnp.float32).astype(jnp.bfloat16)


def gaussian_terms(block, off_x, off_y):
    half = TILE_W // 2 + 0.0
    x = block[0:1] + (off_x - half - 0.5)
    y = block[1:2] + (off_y - half - 0.5)
    a = jnp.exp(block[2:3])
    c = jnp.exp(block[3:4])
    root = jnp.sqrt(a * c)
    b = block[4:5] * root
    return x, y, a, b, c, root


def render_kernel(
    tiles, length, pixels, chunk,
    rows_ref, slot_ref, pad_ref, off_ref, blocks_ref, cot_ref,
    image_ref, out_ref,
    blk, feat_t, coef, basis, basis_t, lower, upper,
    weight, gweight, ratio, moment, dfeat, grads, zero, in_sem, out_sem,
):
    slots = tiles * length
    gauss = blk.shape[2]
    width = blk.shape[1] - ROWS
    pair = 2
    span = pair * gauss
    pairs = length // pair
    chunks = pixels // chunk

    def fetch(s):
        return pltpu.make_async_copy(blocks_ref.at[rows_ref[s]], blk.at[s], in_sem.at[s])

    for s in range(slots):
        fetch(s).start()

    kinds = lax.broadcasted_iota(jnp.int32, basis.shape, 0)
    basis[...] = basis_of(
        lax.broadcasted_iota(jnp.int32, basis.shape, 1), jnp.where(kinds < 24, kinds % 8, 7)
    )
    basis_t[...] = basis_of(
        lax.broadcasted_iota(jnp.int32, basis_t.shape, 0),
        lax.broadcasted_iota(jnp.int32, basis_t.shape, 1),
    )
    row = lax.broadcasted_iota(jnp.int32, lower.shape, 0)
    col = lax.broadcasted_iota(jnp.int32, lower.shape, 1)
    lower[...] = (col < row).astype(jnp.float32).astype(jnp.bfloat16)
    upper[...] = (col > row).astype(jnp.float32).astype(jnp.bfloat16)
    zero[...] = jnp.zeros_like(zero)
    off_x = off_ref[0, 0]
    off_y = off_ref[0, 1]
    for s in range(slots):
        fetch(s).wait()

    def prepare(s, carry):
        block = blk[s, pl.ds(width, ROWS), :].astype(jnp.float32)
        x, y, a, b, c, root = gaussian_terms(block, off_x, off_y)
        tile = s // length
        dead = s - tile * length >= length - pad_ref[0, tile]
        sig = jax.nn.log_sigmoid(block[5:6])
        first = sig - 0.5 * (a * x * x + 2.0 * b * x * y + c * y * y)
        first = jnp.where(dead, -10000.0, first)
        table = jnp.concatenate(
            [first, a * x + b * y, b * x + c * y, -0.5 * a, -b, -0.5 * c,
             jnp.zeros((2, gauss), jnp.float32)], axis=0
        ) * LOG2E
        high = table.astype(jnp.bfloat16).astype(jnp.float32)
        rest = table - high
        mid = rest.astype(jnp.bfloat16).astype(jnp.float32)
        low = rest - mid
        full = jnp.concatenate([high, mid, low, jnp.zeros((8, gauss), jnp.float32)], axis=0)
        coef[pl.ds(pl.multiple_of(s * gauss, gauss), gauss), :] = full.T.astype(jnp.bfloat16)
        return carry

    lax.fori_loop(0, slots, prepare, 0)
    for s in range(slots):
        tile, entry = s // length, s % length
        feat_t[tile, :, entry * gauss:(entry + 1) * gauss] = transposed(blk[s, 0:width, :])

    moment[...] = jnp.zeros_like(moment)
    dfeat[...] = jnp.zeros_like(dfeat)

    def features_of(tile, p):
        first = tile * length + pair * p
        return jnp.concatenate([blk[first + i, 0:width, :] for i in range(pair)], axis=0)

    def step(n, carry):
        tile = n // chunks
        start = pl.multiple_of((n - tile * chunks) * chunk, chunk)
        cot = cot_ref[0, tile, pl.ds(start, chunk), :]
        cot_t = transposed(cot)
        here = basis[:, pl.ds(start, chunk)]
        here_t = basis_t[pl.ds(start, chunk), :]
        log_trans = jnp.zeros((1, chunk), jnp.float32)
        for p in range(pairs):
            rows = slice(p * span, (p + 1) * span)
            base = pl.multiple_of(tile * (length * gauss) + p * span, span)
            alpha = jnp.exp2(f32dot(coef[pl.ds(base, span), :], here))
            keep = 1.0 - alpha
            log_keep = jnp.log2(keep)
            high = log_keep.astype(jnp.bfloat16)
            low = (log_keep - high.astype(jnp.float32)).astype(jnp.bfloat16)
            before = f32dot(lower[...], high) + f32dot(lower[...], low) + log_trans
            w = alpha * jnp.exp2(before)
            log_trans = before[span - 1:span] + log_keep[span - 1:span]
            weight[rows, :] = w.astype(jnp.bfloat16)
            gweight[rows, :] = f32dot(features_of(tile, p), cot_t) * w
            ratio[rows, :] = alpha / keep
        image = f32dot(feat_t[tile], weight[...])
        image_ref[0, tile, pl.ds(start, chunk), :] = image.T.astype(jnp.bfloat16)
        later = jnp.zeros((1, chunk), jnp.float32)
        for p in reversed(range(pairs)):
            rows = slice(p * span, (p + 1) * span)
            base = pl.multiple_of(tile * (length * gauss) + p * span, span)
            gw = gweight[rows, :]
            after = f32dot(upper[...], gw.astype(jnp.bfloat16)) + later
            later = after[0:1] + gw[0:1]
            slope = (gw - after * ratio[rows, :]).astype(jnp.bfloat16)
            moment[pl.ds(base, span), :] += f32dot(slope, here_t)
            dfeat[pl.ds(base, span), :] += f32dot(weight[rows, :], cot)
        return carry

    lax.fori_loop(0, tiles * chunks, step, 0)

    def finish(s, carry):
        base = pl.multiple_of(s * gauss, gauss)
        grads[s, 0:width, :] = dfeat[pl.ds(base, gauss), :].astype(jnp.bfloat16)
        block = blk[s, pl.ds(width, ROWS), :].astype(jnp.float32)
        x, y, a, b, c, root = gaussian_terms(block, off_x, off_y)
        m = moment[pl.ds(base, gauss), :].T
        m0, m1, m2 = m[0:1], m[1:2], m[2:3]
        sx = m1 - x * m0
        sy = m2 - y * m0
        sxx = m[3:4] - 2.0 * x * m1 + x * x * m0
        sxy = m[4:5] - x * m2 - y * m1 + x * y * m0
        syy = m[5:6] - 2.0 * y * m2 + y * y * m0
        table = jnp.concatenate(
            [a * sx + b * sy, b * sx + c * sy,
             -0.5 * (a * sxx + b * sxy), -0.5 * (c * syy + b * sxy),
             -root * sxy, jax.nn.sigmoid(-block[5:6]) * m0,
             jnp.zeros((ROWS - 6, gauss), jnp.float32)], axis=0
        )
        grads[s, pl.ds(width, ROWS), :] = table.astype(jnp.bfloat16)
        return carry

    lax.fori_loop(0, slots, finish, 0)

    spaces = out_ref.shape[0]

    def put(q, carry):
        s = slot_ref[q]

        @pl.when(s >= 0)
        def _():
            pltpu.make_async_copy(grads.at[jnp.maximum(s, 0)], out_ref.at[q], out_sem).start()

        @pl.when(s < 0)
        def _():
            pltpu.make_async_copy(zero, out_ref.at[q], out_sem).start()

        return carry

    lax.fori_loop(0, spaces, put, 0)

    def drain(q, carry):
        pltpu.make_async_copy(zero, out_ref.at[q], out_sem).wait()
        return carry

    lax.fori_loop(0, spaces, drain, 0)


def render(rows, slot_at, pads, offset, blocks, cotangent):
    tiles, pixels = cotangent.shape[1], cotangent.shape[2]
    width, gauss = cotangent.shape[3], blocks.shape[2]
    slots = rows.shape[0]
    length = slots // tiles
    spaces = slot_at.shape[0]
    chunk = 256
    total = slots * gauss
    depth = blocks.shape[1]
    bf, f4 = jnp.bfloat16, jnp.float32
    return pl.pallas_call(
        functools.partial(render_kernel, tiles, length, pixels, chunk),
        out_shape=(
            jax.ShapeDtypeStruct(cotangent.shape, bf),
            jax.ShapeDtypeStruct((spaces, depth, gauss), bf),
        ),
        in_specs=[SMEM, SMEM, SMEM, SMEM, ANY, VMEM],
        out_specs=(VMEM, ANY),
        scratch_shapes=[
            pltpu.VMEM((slots, depth, gauss), bf),
            pltpu.VMEM((tiles, width, length * gauss), bf),
            pltpu.VMEM((total, 32), bf),
            pltpu.VMEM((32, pixels), bf),
            pltpu.VMEM((pixels, 128), bf),
            pltpu.VMEM((2 * gauss, 2 * gauss), bf),
            pltpu.VMEM((2 * gauss, 2 * gauss), bf),
            pltpu.VMEM((length * gauss, chunk), bf),
            pltpu.VMEM((length * gauss, chunk), f4),
            pltpu.VMEM((length * gauss, chunk), f4),
            pltpu.VMEM((total, 128), f4),
            pltpu.VMEM((total, width), f4),
            pltpu.VMEM((slots, depth, gauss), bf),
            pltpu.VMEM((depth, gauss), bf),
            pltpu.SemaphoreType.DMA((slots,)),
            pltpu.SemaphoreType.DMA,
        ],
        compiler_params=pltpu.CompilerParams(vmem_limit_bytes=40 * 2**20),
        name="render",
    )(rows, slot_at, pads, offset, blocks, cotangent)


def plan_kernel(capacity, shard_blocks, list_ref, home_ref, at_ref, slot_ref, req_ref, want, count):
    tile_count = req_ref.shape[0]
    tiles, length = list_ref.shape[1:]
    for o in range(tile_count):
        count[o] = 0

    def clear(q, carry):
        slot_ref[q] = -1
        want[q] = 0
        return carry

    lax.fori_loop(0, tile_count * capacity, clear, 0)

    def place(s, carry):
        tile = s // length
        row = home_ref[list_ref[0, tile, s - tile * length]]
        owner = row // shard_blocks
        rank = count[owner]
        count[owner] = rank + 1
        q = owner * capacity + rank
        at_ref[s] = q
        slot_ref[q] = s
        want[q] = row - owner * shard_blocks + 1
        return carry

    lax.fori_loop(0, tiles * length, place, 0)
    first = lax.axis_index("tile") * capacity
    lane = lax.broadcasted_iota(jnp.int32, req_ref.shape[1:], 1)
    for o in range(tile_count):
        row = jnp.zeros(req_ref.shape[1:], jnp.int32)
        for c in range(capacity):
            row = jnp.where(lane == first + c, want[o * capacity + c], row)
        req_ref[o] = row


def plan(block_list, block_home, tile_count, capacity, shard_blocks):
    slots = block_list.shape[1] * block_list.shape[2]
    spaces = tile_count * capacity
    i4 = jnp.int32
    return pl.pallas_call(
        functools.partial(plan_kernel, capacity, shard_blocks),
        out_shape=(
            jax.ShapeDtypeStruct((slots,), i4),
            jax.ShapeDtypeStruct((spaces,), i4),
            jax.ShapeDtypeStruct((tile_count, 8, 128), i4),
        ),
        in_specs=[SMEM, SMEM],
        out_specs=(SMEM, SMEM, VMEM),
        scratch_shapes=[pltpu.SMEM((spaces,), i4), pltpu.SMEM((tile_count,), i4)],
        name="plan",
    )(block_list, block_home)


def greet(devices):
    barrier = pltpu.get_barrier_semaphore()
    for device in devices:
        pl.semaphore_signal(barrier, inc=1, device_id=device, device_id_type=MESH)
    pl.semaphore_wait(barrier, len(devices))


def remote(src, dst, send, recv, device):
    return pltpu.make_async_remote_copy(
        src_ref=src, dst_ref=dst, send_sem=send, recv_sem=recv,
        device_id=device, device_id_type=MESH,
    )


def fetch_kernel(
    req_ref, centers_ref, scales_ref, corr_ref, opac_ref, feat_ref,
    got_ref, asked_ref,
    req_in, table, par, staged, req_send, req_recv, send, recv, own_sem, table_sem,
):
    tile_count, capacity = got_ref.shape[:2]
    shard_blocks, width, gauss = feat_ref.shape
    me = lax.axis_index("tile")
    peers = [lax.rem(me + d, tile_count) for d in range(tile_count)]
    sources = [lax.rem(me + tile_count - d, tile_count) for d in range(tile_count)]
    greet([{"tile": p} for p in peers[1:]])

    def ask(d):
        return remote(
            req_ref.at[peers[d]], req_in.at[me], req_send.at[d], req_recv.at[me], {"tile": peers[d]}
        )

    def asked_by(d):
        return remote(
            req_ref.at[sources[d]], req_in.at[sources[d]], req_send.at[d],
            req_recv.at[sources[d]], {"tile": sources[d]},
        )

    for d in range(1, tile_count):
        ask(d).start()
    corr = corr_ref[...].astype(jnp.float32)
    opac = opac_ref[...].astype(jnp.float32)
    par[...] = jnp.zeros_like(par)
    for r in range(shard_blocks):
        par[r, 0:2, :] = centers_ref[r].astype(jnp.float32)
        par[r, 2:4, :] = scales_ref[r].astype(jnp.float32)
        par[r, 4:5, :] = corr[r:r + 1]
        par[r, 5:6, :] = opac[r:r + 1]
    wanted = req_ref[me]
    for d in range(1, tile_count):
        asked_by(d).wait_recv()
        wanted = wanted + req_in[sources[d]]
    asked_ref[...] = wanted
    move = pltpu.make_async_copy(asked_ref, table, table_sem)
    move.start()
    move.wait()

    def give(d):
        return remote(staged.at[d], got_ref.at[me], send.at[d], recv.at[me], {"tile": peers[d]})

    def given(d):
        return remote(
            staged.at[d], got_ref.at[sources[d]], send.at[d], recv.at[sources[d]],
            {"tile": sources[d]},
        )

    keep = pltpu.make_async_copy(staged.at[0], got_ref.at[me], own_sem)
    for d in list(range(1, tile_count)) + [0]:
        for c in range(capacity):
            row = jnp.maximum(table[0, peers[d] * capacity + c] - 1, 0)
            staged[d, c, 0:width, :] = feat_ref[row]
            staged[d, c, width:width + ROWS, :] = par[row].astype(jnp.bfloat16)
        if d:
            give(d).start()
        else:
            keep.start()
    keep.wait()
    for d in range(1, tile_count):
        given(d).wait_recv()
    for d in range(1, tile_count):
        give(d).wait_send()
        ask(d).wait_send()


def fetch(req, capacity, centers, log_scales, correlation, opacity_logit, features):
    tile_count = req.shape[0]
    shard_blocks, width, gauss = features.shape
    depth = width + ROWS
    bf = jnp.bfloat16
    dma = pltpu.SemaphoreType.DMA
    return pl.pallas_call(
        fetch_kernel,
        out_shape=(
            jax.ShapeDtypeStruct((tile_count, capacity, depth, gauss), bf),
            jax.ShapeDtypeStruct(req.shape[1:], jnp.int32),
        ),
        in_specs=[VMEM] * 6,
        out_specs=(ANY, VMEM),
        scratch_shapes=[
            pltpu.VMEM(req.shape, jnp.int32),
            pltpu.SMEM(req.shape[1:], jnp.int32),
            pltpu.VMEM((shard_blocks, ROWS, gauss), jnp.float32),
            pltpu.VMEM((tile_count, capacity, depth, gauss), bf),
            dma((tile_count,)), dma((tile_count,)), dma((tile_count,)), dma((tile_count,)),
            dma, dma,
        ],
        compiler_params=pltpu.CompilerParams(
            collective_id=0, has_side_effects=True, vmem_limit_bytes=32 * 2**20
        ),
        name="fetch",
    )(req, centers, log_scales, correlation, opacity_logit, features)


def reduce_kernel(
    shard_blocks, asked_ref, outbound_ref, out_ref,
    landed, total, pair_out, pair_in, chip_out, chip_in, done,
    send, recv, pair_sem, chip_send, chip_recv, done_send, done_recv, mate_send, mate_recv,
):
    tile_count, capacity, depth, gauss = outbound_ref.shape
    cores, chips, part, _ = done.shape
    half = chips * part
    me = lax.axis_index("tile")
    view = lax.axis_index("view")
    core = lax.rem(view, cores)
    chip = view // cores
    mate = {"view": chip * cores + (1 - core)}
    peers = [lax.rem(me + d, tile_count) for d in range(tile_count)]
    sources = [lax.rem(me + tile_count - d, tile_count) for d in range(tile_count)]
    near = [lax.rem(chip + e, chips) for e in range(chips)]
    behind = [lax.rem(chip + chips - e, chips) for e in range(chips)]

    def on_chip(c):
        return {"view": c * cores + core}

    greet([{"tile": p} for p in peers[1:]] + [mate] + [on_chip(c) for c in near[1:]])

    def give(d):
        return remote(
            outbound_ref.at[peers[d]], landed.at[me], send.at[d], recv.at[me], {"tile": peers[d]}
        )

    def given(d):
        return remote(
            outbound_ref.at[sources[d]], landed.at[sources[d]], send.at[d], recv.at[sources[d]],
            {"tile": sources[d]},
        )

    for d in range(1, tile_count):
        give(d).start()
    rows = shard_blocks * depth
    if 2 * half > rows:
        total[rows:2 * half, :] = jnp.zeros((2 * half - rows, gauss), jnp.float32)
    for d in range(tile_count):
        if d:
            given(d).wait_recv()
        place = landed if d else outbound_ref
        source = sources[d]
        marks = [asked_ref[0, source * capacity + c] for c in range(capacity)]

        def add(r, carry):
            at = pl.ds(pl.multiple_of(r * depth, 16), depth)
            acc = total[at, :] if d else jnp.zeros((depth, gauss), jnp.float32)
            for c in range(capacity):
                mark = jnp.where(marks[c] == r + 1, 1.0, 0.0)
                acc = acc + mark * place[source, c].astype(jnp.float32)
            total[at, :] = acc
            return carry

        lax.fori_loop(0, shard_blocks, add, 0)

    def chunk_of(k, c):
        return pl.ds(pl.multiple_of((k * chips + c) * part, 16), part)

    for c in range(chips):
        pair_out[c] = total[chunk_of(1 - core, c), :].astype(jnp.bfloat16)
    pair = remote(pair_out, pair_in, pair_sem.at[0], pair_sem.at[1], mate)
    pair.start()
    pair.wait_recv()

    def to_chip(e):
        return remote(
            chip_out.at[near[e]], chip_in.at[chip], chip_send.at[e], chip_recv.at[chip],
            on_chip(near[e]),
        )

    def from_chip(e):
        return remote(
            chip_out.at[behind[e]], chip_in.at[behind[e]], chip_send.at[e],
            chip_recv.at[behind[e]], on_chip(behind[e]),
        )

    for e in range(1, chips):
        c = near[e]
        chip_out[c] = (
            total[chunk_of(core, c), :] + pair_in[c].astype(jnp.float32)
        ).astype(jnp.bfloat16)
        to_chip(e).start()
    mine = total[chunk_of(core, chip), :] + pair_in[chip].astype(jnp.float32)
    for e in range(1, chips):
        from_chip(e).wait_recv()
        mine = mine + chip_in[behind[e]].astype(jnp.float32)
    done[core, chip] = mine.astype(jnp.bfloat16)

    def spread(e):
        return remote(
            done.at[core, chip], done.at[core, chip], done_send.at[e], done_recv.at[chip],
            on_chip(near[e]),
        )

    def spread_from(e):
        c = behind[e]
        return remote(
            done.at[core, c], done.at[core, c], done_send.at[e], done_recv.at[c], on_chip(c)
        )

    def pass_on(c):
        return remote(done.at[core, c], done.at[core, c], mate_send.at[c], mate_recv.at[c], mate)

    def passed(c):
        return remote(
            done.at[1 - core, c], done.at[1 - core, c], mate_send.at[c], mate_recv.at[c], mate
        )

    for e in range(1, chips):
        spread(e).start()
    pass_on(chip).start()
    for e in range(1, chips):
        spread_from(e).wait_recv()
        pass_on(behind[e]).start()
    for e in range(chips):
        passed(behind[e]).wait_recv()
    for k in range(cores):
        for c in range(chips):
            out_ref[k, c] = done[k, c]
    for e in range(chips):
        pass_on(behind[e]).wait_send()
    for e in range(1, chips):
        spread(e).wait_send()
        to_chip(e).wait_send()
    pair.wait_send()
    for d in range(1, tile_count):
        give(d).wait_send()


def reduce_grads(asked, outbound, shard_blocks, views):
    tile_count, capacity, depth, gauss = outbound.shape
    cores = 2
    chips = views // cores
    part = -(-shard_blocks * depth // (views * 16)) * 16
    bf, f4 = jnp.bfloat16, jnp.float32
    dma = pltpu.SemaphoreType.DMA
    return pl.pallas_call(
        functools.partial(reduce_kernel, shard_blocks),
        out_shape=jax.ShapeDtypeStruct((cores, chips, part, gauss), bf),
        in_specs=[SMEM, VMEM],
        out_specs=VMEM,
        scratch_shapes=[
            pltpu.VMEM(outbound.shape, bf),
            pltpu.VMEM((views * part, gauss), f4),
            pltpu.VMEM((chips, part, gauss), bf),
            pltpu.VMEM((chips, part, gauss), bf),
            pltpu.VMEM((chips, part, gauss), bf),
            pltpu.VMEM((chips, part, gauss), bf),
            pltpu.VMEM((cores, chips, part, gauss), bf),
            dma((tile_count,)), dma((tile_count,)), dma((2,)),
            dma((chips,)), dma((chips,)), dma((chips,)), dma((chips,)),
            dma((chips,)), dma((chips,)),
        ],
        compiler_params=pltpu.CompilerParams(
            collective_id=1, has_side_effects=True, vmem_limit_bytes=32 * 2**20
        ),
        name="reduce_grads",
    )(asked, outbound)


def unpack_kernel(all_ref, centers_ref, scales_ref, corr_ref, opac_ref, feat_ref):
    shard_blocks, width, _ = feat_ref.shape
    depth = width + ROWS
    for r in range(shard_blocks):
        feat_ref[r] = all_ref[r * depth:r * depth + width, :].astype(jnp.float32)
        par = all_ref[r * depth + width:(r + 1) * depth, :].astype(jnp.float32)
        centers_ref[r] = par[0:2]
        scales_ref[r] = par[2:4]
        corr_ref[r:r + 1, :] = par[4:5]
        opac_ref[r:r + 1, :] = par[5:6]


def unpack(everything, shard_blocks, width, gauss):
    f4 = jnp.float32
    return pl.pallas_call(
        unpack_kernel,
        out_shape=(
            jax.ShapeDtypeStruct((shard_blocks, 2, gauss), f4),
            jax.ShapeDtypeStruct((shard_blocks, 2, gauss), f4),
            jax.ShapeDtypeStruct((shard_blocks, gauss), f4),
            jax.ShapeDtypeStruct((shard_blocks, gauss), f4),
            jax.ShapeDtypeStruct((shard_blocks, width, gauss), f4),
        ),
        in_specs=[VMEM],
        out_specs=(VMEM,) * 5,
        compiler_params=pltpu.CompilerParams(vmem_limit_bytes=32 * 2**20),
        name="unpack",
    )(everything)


def shards(
    centers, log_scales, correlation, opacity_logit, features,
    view_offset, block_list, pad_count, block_home, image_grad,
):
    tile_count = lax.axis_size("tile")
    views = lax.axis_size("view")
    shard_blocks, _, gauss = centers.shape
    width = features.shape[2]
    slot_count = block_list.shape[1] * block_list.shape[2]
    capacity = (slot_count + tile_count - 1) // tile_count + 1
    place, slot_at, req = plan(block_list, block_home, tile_count, capacity, shard_blocks)
    got, asked = fetch(
        req, capacity, centers, log_scales, correlation, opacity_logit, features
    )
    blocks = got.reshape((tile_count * capacity,) + got.shape[2:])
    image, outbound = render(place, slot_at, pad_count, view_offset, blocks, image_grad)
    summed = reduce_grads(asked, outbound.reshape(got.shape), shard_blocks, views)
    return (image,) + tuple(unpack(summed.reshape(-1, gauss), shard_blocks, width, gauss))


def solution(mesh):
    in_specs = (
        P("tile", None, None),
        P("tile", None, None),
        P("tile", None),
        P("tile", None),
        P("tile", None, None),
        P("view", None),
        P("view", "tile", None),
        P("view", "tile"),
        P(),
        P("view", "tile", None, None),
    )
    out_specs = (
        P("view", "tile", None, None),
        P("tile", None, None),
        P("tile", None, None),
        P("tile", None),
        P("tile", None),
        P("tile", None, None),
    )
    return jax.shard_map(shards, mesh=mesh, in_specs=in_specs, out_specs=out_specs, check_vma=False)
```

```python
import functools

import jax
import jax.numpy as jnp
from jax import lax
from jax.experimental import pallas as pl
from jax.experimental.pallas import tpu as pltpu
from jax.sharding import PartitionSpec as P

TILE_W = 32
ROWS = 16
PAIR = 2
CORES = 2
LOG2E = 1.4426950408889634
SMEM = pl.BlockSpec(memory_space=pltpu.SMEM)
VMEM = pl.BlockSpec(memory_space=pltpu.VMEM)
ANY = pl.BlockSpec(memory_space=pl.ANY)
MESH = pl.DeviceIdType.MESH


def f32dot(a, b):
    return jnp.dot(a, b, preferred_element_type=jnp.float32)


def transposed(a):
    return a.astype(jnp.float32).T.astype(a.dtype)


def basis_of(pixel, kind):
    half = TILE_W // 2
    k = pixel % TILE_W - half
    j = pixel // TILE_W - half
    out = jnp.where(kind == 0, 1, 0)
    out = jnp.where(kind == 1, k, out)
    out = jnp.where(kind == 2, j, out)
    out = jnp.where(kind == 3, k * k, out)
    out = jnp.where(kind == 4, k * j, out)
    out = jnp.where(kind == 5, j * j, out)
    return out.astype(jnp.float32).astype(jnp.bfloat16)


def gaussian_terms(block, off_x, off_y):
    half = TILE_W // 2 + 0.0
    x = block[0:1] + (off_x - half - 0.5)
    y = block[1:2] + (off_y - half - 0.5)
    a = jnp.exp(block[2:3])
    c = jnp.exp(block[3:4])
    root = jnp.sqrt(a * c)
    b = block[4:5] * root
    return x, y, a, b, c, root


def remote(src, dst, send, recv, device):
    return pltpu.make_async_remote_copy(
        src_ref=src, dst_ref=dst, send_sem=send, recv_sem=recv,
        device_id=device, device_id_type=MESH,
    )


def local(src, dst, sem):
    return pltpu.make_async_copy(src, dst, sem)


def splat_kernel(
    capacity, chunk,
    list_hbm, home_hbm, pad_hbm, off_hbm, centers_hbm, scales_hbm, corr_hbm, opac_hbm,
    feat_hbm, cot_hbm,
    image_ref, out_ref,
    list_ref, home_ref, pad_ref, off_ref, centers_ref, scales_ref, corr_ref, opac_ref,
    feat_ref, cot_ref, in_sem,
    at_ref, owner_ref, slot_ref, req, req_in, table_v, table, table_sem, req_send, req_recv,
    par, par_out, par_in, feat_out, feat_in,
    par_send, par_recv, feat_send, feat_recv,
    blk, prm, feat_t, coef, basis, basis_t, lower, upper,
    weight, exact, ratio, moment, dfeat, dpar,
    grad_out, grad_in, dpar_out, dpar_in, grad_send, grad_recv, dpar_send, dpar_recv,
    total, pair_out, pair_in, chip_out, chip_in, done,
    pair_sem, chip_send, chip_recv, done_send, done_recv, mate_send, mate_recv,
):
    _, tiles, length = list_ref.shape
    pixels = cot_ref.shape[2]
    slots = tiles * length
    shard_blocks, gauss, width = feat_ref.shape
    tile_count = req.shape[0]
    depth = gauss + ROWS
    span = PAIR * gauss
    pairs = length // PAIR
    chunks = pixels // chunk
    _, chips, part, _ = done.shape
    half = chips * part
    bf, f4 = jnp.bfloat16, jnp.float32

    me = lax.axis_index("tile")
    view = lax.axis_index("view")
    core = lax.rem(view, CORES)
    chip = view // CORES
    mate = {"view": chip * CORES + (1 - core)}
    peers = [lax.rem(me + d, tile_count) for d in range(tile_count)]
    sources = [lax.rem(me + tile_count - d, tile_count) for d in range(tile_count)]
    near = [lax.rem(chip + e, chips) for e in range(chips)]
    behind = [lax.rem(chip + chips - e, chips) for e in range(chips)]

    def on_chip(c):
        return {"view": c * CORES + core}

    def give(out, into, send, recv, d):
        return remote(out.at[peers[d]], into.at[me], send.at[d], recv.at[me], {"tile": peers[d]})

    def given(out, into, send, recv, d):
        s = sources[d]
        return remote(out.at[s], into.at[s], send.at[d], recv.at[s], {"tile": s})

    ask = (req, req_in, req_send, req_recv)
    pars = (par_out, par_in, par_send, par_recv)
    feats = (feat_out, feat_in, feat_send, feat_recv)
    grads = (grad_out, grad_in, grad_send, grad_recv)
    dpars = (dpar_out, dpar_in, dpar_send, dpar_recv)

    loads = [
        local(src, dst, in_sem.at[n]) for n, (src, dst) in enumerate((
            (list_hbm, list_ref), (home_hbm, home_ref), (pad_hbm, pad_ref), (off_hbm, off_ref),
            (centers_hbm, centers_ref), (scales_hbm, scales_ref), (corr_hbm, corr_ref),
            (opac_hbm, opac_ref), (feat_hbm, feat_ref), (cot_hbm, cot_ref),
        ))
    ]
    for load in loads:
        load.start()
    barrier = pltpu.get_barrier_semaphore()
    others = [{"tile": p} for p in peers[1:]] + [mate] + [on_chip(c) for c in near[1:]]
    for device in others:
        pl.semaphore_signal(barrier, inc=1, device_id=device, device_id_type=MESH)

    loads[0].wait()
    loads[1].wait()
    first = me * capacity
    lane = lax.broadcasted_iota(jnp.int32, req.shape[1:], 1)
    asks = [jnp.zeros(req.shape[1:], jnp.int32) for _ in range(tile_count)]
    owners, places = [], []
    for s in range(slots):
        row = home_ref[list_ref[0, s // length, s % length]]
        owner = row // shard_blocks
        rank = jnp.int32(0)
        for other in owners:
            rank = rank + jnp.where(other == owner, 1, 0)
        owners.append(owner)
        places.append(owner * capacity + rank)
        at_ref[s] = places[s]
        for o in range(tile_count):
            here = jnp.where(owner == o, row - owner * shard_blocks + 1, 0)
            asks[o] = asks[o] + jnp.where(lane == first + rank, here, 0)
    for o in range(tile_count):
        req[o] = asks[o]
    pl.semaphore_wait(barrier, len(others))
    for d in range(1, tile_count):
        give(*ask, d).start()

    for load in loads[2:]:
        load.wait()
    corr = corr_ref[...].astype(f4)
    opac = opac_ref[...].astype(f4)
    par[...] = jnp.zeros_like(par)
    for r in range(shard_blocks):
        par[r, 0:2, :] = centers_ref[r].astype(f4)
        par[r, 2:4, :] = scales_ref[r].astype(f4)
        par[r, 4:5, :] = corr[r:r + 1]
        par[r, 5:6, :] = opac[r:r + 1]
    wanted = req[me]
    for d in range(1, tile_count):
        given(*ask, d).wait_recv()
        wanted = wanted + req_in[sources[d]]
    table_v[...] = wanted
    move = local(table_v, table, table_sem)
    move.start()
    move.wait()

    def wanted_row(d, c):
        return jnp.maximum(table[0, peers[d] * capacity + c] - 1, 0)

    for d in range(1, tile_count):
        for c in range(capacity):
            par_out[peers[d], c] = par[wanted_row(d, c)].astype(bf)
        give(*pars, d).start()
    for d in range(1, tile_count):
        for c in range(capacity):
            feat_out[peers[d], c] = feat_ref[wanted_row(d, c)]
        give(*feats, d).start()
    for c in range(capacity):
        par_in[me, c] = par[wanted_row(0, c)].astype(bf)
        feat_in[me, c] = feat_ref[wanted_row(0, c)]

    kinds = lax.broadcasted_iota(jnp.int32, basis.shape, 0)
    basis[...] = basis_of(
        lax.broadcasted_iota(jnp.int32, basis.shape, 1), jnp.where(kinds < 24, kinds % 8, 7)
    )
    basis_t[...] = basis_of(
        lax.broadcasted_iota(jnp.int32, basis_t.shape, 0),
        lax.broadcasted_iota(jnp.int32, basis_t.shape, 1),
    )
    across = lax.broadcasted_iota(jnp.int32, lower.shape, 0)
    along = lax.broadcasted_iota(jnp.int32, lower.shape, 1)
    lower[...] = (along < across).astype(f4).astype(bf)
    upper[...] = (along > across).astype(f4).astype(bf)
    moment[...] = jnp.zeros_like(moment)
    dfeat[...] = jnp.zeros_like(dfeat)
    for q in range(tile_count * capacity):
        slot = jnp.int32(0)
        for s in range(slots):
            slot = slot + jnp.where(places[s] == q, s + 1, 0)
        slot_ref[q] = slot
    off_x = off_ref[0, 0]
    off_y = off_ref[0, 1]

    def entry(ref, s):
        q = at_ref[s]
        owner = q // capacity
        return ref[owner, q - owner * capacity]

    for d in range(1, tile_count):
        given(*pars, d).wait_recv()

    def prepare(s, carry):
        block = entry(par_in, s).astype(f4)
        prm[s] = block
        x, y, a, b, c, root = gaussian_terms(block, off_x, off_y)
        tile = s // length
        dead = s - tile * length >= length - pad_ref[0, tile]
        sig = jax.nn.log_sigmoid(block[5:6])
        const = sig - 0.5 * (a * x * x + 2.0 * b * x * y + c * y * y)
        const = jnp.where(dead, -10000.0, const)
        terms = jnp.concatenate(
            [const, a * x + b * y, b * x + c * y, -0.5 * a, -b, -0.5 * c,
             jnp.zeros((2, gauss), f4)], axis=0
        ) * LOG2E
        high = terms.astype(bf).astype(f4)
        rest = terms - high
        mid = rest.astype(bf).astype(f4)
        full = jnp.concatenate([high, mid, rest - mid, jnp.zeros((8, gauss), f4)], axis=0)
        coef[pl.ds(pl.multiple_of(s * gauss, gauss), gauss), :] = full.T.astype(bf)
        return carry

    lax.fori_loop(0, slots, prepare, 0)

    def forward(n, carry):
        tile = n // chunks
        start = pl.multiple_of((n - tile * chunks) * chunk, chunk)
        cot = cot_ref[0, tile, pl.ds(start, chunk), :]
        here = basis[:, pl.ds(start, chunk)]
        log_trans = jnp.zeros((1, chunk), f4)
        for p in range(pairs):
            base = pl.multiple_of(tile * (length * gauss) + p * span, span)
            at = (n, pl.ds(p * span, span))
            alpha = jnp.exp2(f32dot(coef[pl.ds(base, span), :], here))
            keep = 1.0 - alpha
            log_keep = jnp.log2(keep)
            high = log_keep.astype(bf)
            low = (log_keep - high.astype(f4)).astype(bf)
            before = f32dot(lower[...], high) + f32dot(lower[...], low) + log_trans
            w = alpha * jnp.exp2(before)
            log_trans = before[span - 1:span] + log_keep[span - 1:span]
            wb = w.astype(bf)
            weight[at] = wb
            exact[at] = w
            ratio[at] = alpha / keep
            slot = tile * length + p * PAIR
            more = f32dot(wb, cot)
            for i in range(PAIR):
                dfeat[slot + i] += more[i * gauss:(i + 1) * gauss]
        return carry

    lax.fori_loop(0, tiles * chunks, forward, 0)

    def outgoing(grad_ref, q):
        slot = slot_ref[q]
        return jnp.where(slot > 0, grad_ref[jnp.maximum(slot - 1, 0)], 0.0)

    for d in list(range(1, tile_count)) + [0]:
        for c in range(capacity):
            got = outgoing(dfeat, peers[d] * capacity + c).astype(bf)
            if d:
                grad_out[peers[d], c] = got
            else:
                grad_in[me, c] = got
        if d:
            give(*grads, d).start()

    for d in range(1, tile_count):
        given(*feats, d).wait_recv()
    for s in range(slots):
        tile, place = s // length, s % length
        feature = entry(feat_in, s)
        blk[s] = feature
        feat_t[tile, :, place * gauss:(place + 1) * gauss] = transposed(feature)

    def backward(n, carry):
        tile = n // chunks
        start = pl.multiple_of((n - tile * chunks) * chunk, chunk)
        cot_t = transposed(cot_ref[0, tile, pl.ds(start, chunk), :])
        here_t = basis_t[pl.ds(start, chunk), :]
        later = jnp.zeros((1, chunk), f4)
        for p in reversed(range(pairs)):
            base = pl.multiple_of(tile * (length * gauss) + p * span, span)
            at = (n, pl.ds(p * span, span))
            slot = tile * length + p * PAIR
            feature = jnp.concatenate([blk[slot + i] for i in range(PAIR)], axis=0)
            gw = f32dot(feature, cot_t) * exact[at]
            after = f32dot(upper[...], gw.astype(bf)) + later
            later = after[0:1] + gw[0:1]
            slope = (gw - after * ratio[at]).astype(bf)
            moment[pl.ds(base, span), :] += f32dot(slope, here_t)
        image = f32dot(feat_t[tile], weight[n])
        image_ref[0, tile, pl.ds(start, chunk), :] = image.T.astype(bf)
        return carry

    lax.fori_loop(0, tiles * chunks, backward, 0)

    def finish(s, carry):
        x, y, a, b, c, root = gaussian_terms(prm[s], off_x, off_y)
        m = moment[pl.ds(pl.multiple_of(s * gauss, gauss), gauss), :].T
        m0, m1, m2 = m[0:1], m[1:2], m[2:3]
        sx = m1 - x * m0
        sy = m2 - y * m0
        sxx = m[3:4] - 2.0 * x * m1 + x * x * m0
        sxy = m[4:5] - x * m2 - y * m1 + x * y * m0
        syy = m[5:6] - 2.0 * y * m2 + y * y * m0
        dpar[s] = jnp.concatenate(
            [a * sx + b * sy, b * sx + c * sy,
             -0.5 * (a * sxx + b * sxy), -0.5 * (c * syy + b * sxy),
             -root * sxy, jax.nn.sigmoid(-prm[s, 5:6, :]) * m0,
             jnp.zeros((2, gauss), f4)], axis=0
        )
        return carry

    lax.fori_loop(0, slots, finish, 0)
    for d in list(range(1, tile_count)) + [0]:
        for c in range(capacity):
            got = outgoing(dpar, peers[d] * capacity + c)
            if d:
                dpar_out[peers[d], c] = got
            else:
                dpar_in[me, c] = got
        if d:
            give(*dpars, d).start()

    total[...] = jnp.zeros_like(total)
    for d in range(tile_count):
        if d:
            given(*grads, d).wait_recv()
        source = sources[d]
        marks = [table[0, source * capacity + c] for c in range(capacity)]

        def add(r, carry):
            at = pl.ds(pl.multiple_of(r * depth, 16), gauss)
            acc = total[at, :]
            for c in range(capacity):
                mark = jnp.where(marks[c] == r + 1, 1.0, 0.0)
                acc = acc + mark * grad_in[source, c].astype(f4)
            total[at, :] = acc
            return carry

        lax.fori_loop(0, shard_blocks, add, 0)
    for d in range(1, tile_count):
        given(*dpars, d).wait_recv()

    def add_par(r, carry):
        acc = jnp.zeros(dpar_in.shape[2:], f4)
        for t in range(tile_count):
            for c in range(capacity):
                mark = jnp.where(table[0, t * capacity + c] == r + 1, 1.0, 0.0)
                acc = acc + mark * dpar_in[t, c]
        total[pl.ds(pl.multiple_of(r * depth + gauss, 16), 8), :] = acc
        return carry

    lax.fori_loop(0, shard_blocks, add_par, 0)

    def chunk_of(k, c):
        return pl.ds(pl.multiple_of((k * chips + c) * part, 16), part)

    for c in range(chips):
        pair_out[c] = total[chunk_of(1 - core, c), :].astype(bf)
    pair = remote(pair_out, pair_in, pair_sem.at[0], pair_sem.at[1], mate)
    pair.start()
    pair.wait_recv()

    def to_chip(e):
        return remote(
            chip_out.at[near[e]], chip_in.at[chip], chip_send.at[e], chip_recv.at[chip],
            on_chip(near[e]),
        )

    def from_chip(e):
        return remote(
            chip_out.at[behind[e]], chip_in.at[behind[e]], chip_send.at[e],
            chip_recv.at[behind[e]], on_chip(behind[e]),
        )

    for e in range(1, chips):
        c = near[e]
        chip_out[c] = (total[chunk_of(core, c), :] + pair_in[c].astype(f4)).astype(bf)
        to_chip(e).start()
    mine = total[chunk_of(core, chip), :] + pair_in[chip].astype(f4)
    for e in range(1, chips):
        from_chip(e).wait_recv()
        mine = mine + chip_in[behind[e]].astype(f4)
    done[core, chip] = mine.astype(bf)

    def spread(e):
        return remote(
            done.at[core, chip], done.at[core, chip], done_send.at[e], done_recv.at[chip],
            on_chip(near[e]),
        )

    def spread_from(e):
        c = behind[e]
        return remote(
            done.at[core, c], done.at[core, c], done_send.at[e], done_recv.at[c], on_chip(c)
        )

    def pass_on(c):
        return remote(done.at[core, c], done.at[core, c], mate_send.at[c], mate_recv.at[c], mate)

    def passed(c):
        return remote(
            done.at[1 - core, c], done.at[1 - core, c], mate_send.at[c], mate_recv.at[c], mate
        )

    for e in range(1, chips):
        spread(e).start()
    pass_on(chip).start()
    for e in range(1, chips):
        spread_from(e).wait_recv()
        pass_on(behind[e]).start()
    for e in range(chips):
        passed(behind[e]).wait_recv()
    for k in range(CORES):
        for c in range(chips):
            out_ref[k, c] = done[k, c]
    for e in range(chips):
        pass_on(behind[e]).wait_send()
    for e in range(1, chips):
        spread(e).wait_send()
        to_chip(e).wait_send()
    pair.wait_send()
    for d in range(1, tile_count):
        for buffers in (ask, pars, feats, grads, dpars):
            give(*buffers, d).wait_send()


def splat(
    block_list, block_home, pads, offset, centers, log_scales, correlation, opacity_logit,
    features, cotangent, tile_count, views, capacity,
):
    _, tiles, pixels, width = cotangent.shape
    shard_blocks, gauss, _ = features.shape
    length = block_list.shape[2]
    slots = tiles * length
    spaces = tile_count * capacity
    chunk = 256
    steps = tiles * (pixels // chunk)
    total = slots * gauss
    depth = gauss + ROWS
    chips = views // CORES
    part = -(-shard_blocks * depth // (views * 16)) * 16
    bf, f4, i4 = jnp.bfloat16, jnp.float32, jnp.int32
    dma = pltpu.SemaphoreType.DMA
    each = dma((tile_count,))
    args = (
        block_list, block_home, pads, offset, centers, log_scales, correlation, opacity_logit,
        features, cotangent,
    )
    held = [pltpu.SMEM(a.shape, a.dtype) for a in args[:4]]
    held += [pltpu.VMEM(a.shape, a.dtype) for a in args[4:]]
    held += [dma((len(args),))]
    held += [
        pltpu.SMEM((slots,), i4), pltpu.SMEM((slots,), i4), pltpu.SMEM((spaces,), i4),
        pltpu.VMEM((tile_count, 8, 128), i4), pltpu.VMEM((tile_count, 8, 128), i4),
        pltpu.VMEM((8, 128), i4), pltpu.SMEM((8, 128), i4), dma, each, each,
        pltpu.VMEM((shard_blocks, ROWS, gauss), f4),
    ]
    held += [pltpu.VMEM((tile_count, capacity, ROWS, gauss), bf)] * 2
    held += [pltpu.VMEM((tile_count, capacity, gauss, width), bf)] * 2
    held += [each] * 4
    held += [
        pltpu.VMEM((slots, gauss, width), bf),
        pltpu.VMEM((slots, ROWS, gauss), f4),
        pltpu.VMEM((tiles, width, length * gauss), bf),
        pltpu.VMEM((total, 32), bf),
        pltpu.VMEM((32, pixels), bf),
        pltpu.VMEM((pixels, 128), bf),
        pltpu.VMEM((PAIR * gauss, PAIR * gauss), bf),
        pltpu.VMEM((PAIR * gauss, PAIR * gauss), bf),
        pltpu.VMEM((steps, length * gauss, chunk), bf),
        pltpu.VMEM((steps, length * gauss, chunk), f4),
        pltpu.VMEM((steps, length * gauss, chunk), f4),
        pltpu.VMEM((total, 128), f4),
        pltpu.VMEM((slots, gauss, width), f4),
        pltpu.VMEM((slots, 8, gauss), f4),
    ]
    held += [pltpu.VMEM((tile_count, capacity, gauss, width), bf)] * 2
    held += [pltpu.VMEM((tile_count, capacity, 8, gauss), f4)] * 2
    held += [each] * 4
    held += [pltpu.VMEM((views * part, gauss), f4)]
    held += [pltpu.VMEM((chips, part, gauss), bf)] * 4
    held += [pltpu.VMEM((CORES, chips, part, gauss), bf)]
    held += [dma((2,))] + [dma((chips,))] * 6
    return pl.pallas_call(
        functools.partial(splat_kernel, capacity, chunk),
        out_shape=(
            jax.ShapeDtypeStruct(cotangent.shape, bf),
            jax.ShapeDtypeStruct((CORES, chips, part, gauss), bf),
        ),
        in_specs=[ANY] * len(args),
        out_specs=(VMEM, VMEM),
        scratch_shapes=held,
        compiler_params=pltpu.CompilerParams(
            collective_id=0, has_side_effects=True, vmem_limit_bytes=58 * 2**20
        ),
        name="splat",
    )(*args)


def unpack_kernel(all_ref, centers_ref, scales_ref, corr_ref, opac_ref, feat_ref):
    shard_blocks, width, _ = feat_ref.shape
    depth = width + ROWS
    for r in range(shard_blocks):
        feat_ref[r] = all_ref[r * depth:r * depth + width, :].astype(jnp.float32)
        par = all_ref[r * depth + width:(r + 1) * depth, :].astype(jnp.float32)
        centers_ref[r] = par[0:2]
        scales_ref[r] = par[2:4]
        corr_ref[r:r + 1, :] = par[4:5]
        opac_ref[r:r + 1, :] = par[5:6]


def unpack(everything, shard_blocks, width, gauss):
    f4 = jnp.float32
    return pl.pallas_call(
        unpack_kernel,
        out_shape=(
            jax.ShapeDtypeStruct((shard_blocks, 2, gauss), f4),
            jax.ShapeDtypeStruct((shard_blocks, 2, gauss), f4),
            jax.ShapeDtypeStruct((shard_blocks, gauss), f4),
            jax.ShapeDtypeStruct((shard_blocks, gauss), f4),
            jax.ShapeDtypeStruct((shard_blocks, width, gauss), f4),
        ),
        in_specs=[VMEM],
        out_specs=(VMEM,) * 5,
        compiler_params=pltpu.CompilerParams(vmem_limit_bytes=32 * 2**20),
        name="unpack",
    )(everything)


def shards(
    centers, log_scales, correlation, opacity_logit, features,
    view_offset, block_list, pad_count, block_home, image_grad,
):
    tile_count = lax.axis_size("tile")
    views = lax.axis_size("view")
    shard_blocks, gauss, width = features.shape
    slot_count = block_list.shape[1] * block_list.shape[2]
    capacity = (slot_count + tile_count - 1) // tile_count + 1
    image, summed = splat(
        block_list, block_home, pad_count, view_offset, centers, log_scales, correlation,
        opacity_logit, features, image_grad, tile_count, views, capacity,
    )
    return (image,) + tuple(unpack(summed.reshape(-1, gauss), shard_blocks, width, gauss))


def solution(mesh):
    in_specs = (
        P("tile", None, None),
        P("tile", None, None),
        P("tile", None),
        P("tile", None),
        P("tile", None, None),
        P("view", None),
        P("view", "tile", None),
        P("view", "tile"),
        P(),
        P("view", "tile", None, None),
    )
    out_specs = (
        P("view", "tile", None, None),
        P("tile", None, None),
        P("tile", None, None),
        P("tile", None),
        P("tile", None),
        P("tile", None, None),
    )
    return jax.shard_map(shards, mesh=mesh, in_specs=in_specs, out_specs=out_specs, check_vma=False)
```

```python
import functools

import jax
import jax.numpy as jnp
from jax import lax
from jax.experimental import pallas as pl
from jax.experimental.pallas import tpu as pltpu
from jax.sharding import PartitionSpec as P

TILE_W = 32
ROWS = 16
PAIR = 2
CORES = 2
PIECES = 4
LOG2E = 1.4426950408889634
SMEM = pl.BlockSpec(memory_space=pltpu.SMEM)
VMEM = pl.BlockSpec(memory_space=pltpu.VMEM)
ANY = pl.BlockSpec(memory_space=pl.ANY)
MESH = pl.DeviceIdType.MESH


def f32dot(a, b):
    return jnp.dot(a, b, preferred_element_type=jnp.float32)


def transposed(a):
    return a.astype(jnp.float32).T.astype(a.dtype)


def basis_of(pixel, kind):
    half = TILE_W // 2
    k = pixel % TILE_W - half
    j = pixel // TILE_W - half
    out = jnp.where(kind == 0, 1, 0)
    out = jnp.where(kind == 1, k, out)
    out = jnp.where(kind == 2, j, out)
    out = jnp.where(kind == 3, k * k, out)
    out = jnp.where(kind == 4, k * j, out)
    out = jnp.where(kind == 5, j * j, out)
    return out.astype(jnp.float32).astype(jnp.bfloat16)


def gaussian_terms(block, off_x, off_y):
    half = TILE_W // 2 + 0.0
    x = block[0:1] + (off_x - half - 0.5)
    y = block[1:2] + (off_y - half - 0.5)
    a = jnp.exp(block[2:3])
    c = jnp.exp(block[3:4])
    root = jnp.sqrt(a * c)
    b = block[4:5] * root
    return x, y, a, b, c, root


def remote(src, dst, send, recv, device):
    return pltpu.make_async_remote_copy(
        src_ref=src, dst_ref=dst, send_sem=send, recv_sem=recv,
        device_id=device, device_id_type=MESH,
    )


def local(src, dst, sem):
    return pltpu.make_async_copy(src, dst, sem)


def splat_kernel(
    capacity, chunk,
    list_hbm, home_hbm, pad_hbm, off_hbm, centers_hbm, scales_hbm, corr_hbm, opac_hbm,
    feat_hbm, cot_hbm,
    image_ref, out_ref, out_par_ref,
    list_ref, home_ref, pad_ref, off_ref, centers_ref, scales_ref, corr_ref, opac_ref,
    feat_ref, cot_ref, in_sem,
    at_ref, owner_ref, slot_ref, req, req_in, table_v, table, table_sem, req_send, req_recv,
    par, par_out, par_in, feat_out, feat_in,
    par_send, par_recv, feat_send, feat_recv,
    blk, prm, feat_t, coef, basis, basis_t, lower, upper,
    weight, exact, ratio, moment, dfeat, dpar,
    grad_out, grad_in, dpar_out, dpar_in, grad_send, grad_recv, dpar_send, dpar_recv,
    total, pair_out, pair_in, chip_out, chip_in, done,
    total_p, pair_out_p, pair_in_p, chip_out_p, chip_in_p, done_p,
    pair_sem, chip_send, chip_recv, done_send, done_recv, mate_send, mate_recv,
):
    _, tiles, length = list_ref.shape
    pixels = cot_ref.shape[2]
    slots = tiles * length
    shard_blocks, gauss, width = feat_ref.shape
    tile_count = req.shape[0]
    span = PAIR * gauss
    pairs = length // PAIR
    chunks = pixels // chunk
    steps = tiles * chunks
    chips = done.shape[2]
    piece = gauss // PIECES
    bf, f4 = jnp.bfloat16, jnp.float32

    me = lax.axis_index("tile")
    view = lax.axis_index("view")
    core = lax.rem(view, CORES)
    chip = view // CORES
    mate = {"view": chip * CORES + (1 - core)}
    peers = [lax.rem(me + d, tile_count) for d in range(tile_count)]
    sources = [lax.rem(me + tile_count - d, tile_count) for d in range(tile_count)]
    near = [lax.rem(chip + e, chips) for e in range(chips)]
    behind = [lax.rem(chip + chips - e, chips) for e in range(chips)]

    def on_chip(c):
        return {"view": c * CORES + core}

    def give(out, into, send, recv, d):
        return remote(out.at[peers[d]], into.at[me], send.at[d], recv.at[me], {"tile": peers[d]})

    def given(out, into, send, recv, d):
        s = sources[d]
        return remote(out.at[s], into.at[s], send.at[d], recv.at[s], {"tile": s})

    ask = (req, req_in, req_send, req_recv)
    pars = (par_out, par_in, par_send, par_recv)
    feats = (feat_out, feat_in, feat_send, feat_recv)
    grads = [
        tuple(ref.at[k] for ref in (grad_out, grad_in, grad_send, grad_recv))
        for k in range(PIECES)
    ]
    dpars = (dpar_out, dpar_in, dpar_send, dpar_recv)

    loads = [
        local(src, dst, in_sem.at[n]) for n, (src, dst) in enumerate((
            (list_hbm, list_ref), (home_hbm, home_ref), (pad_hbm, pad_ref), (off_hbm, off_ref),
            (centers_hbm, centers_ref), (scales_hbm, scales_ref), (corr_hbm, corr_ref),
            (opac_hbm, opac_ref), (feat_hbm, feat_ref), (cot_hbm, cot_ref),
        ))
    ]
    for load in loads:
        load.start()
    barrier = pltpu.get_barrier_semaphore()
    others = [{"tile": p} for p in peers[1:]] + [mate] + [on_chip(c) for c in near[1:]]
    for device in others:
        pl.semaphore_signal(barrier, inc=1, device_id=device, device_id_type=MESH)

    loads[0].wait()
    loads[1].wait()
    first = me * capacity
    lane = lax.broadcasted_iota(jnp.int32, req.shape[1:], 1)
    asks = [jnp.zeros(req.shape[1:], jnp.int32) for _ in range(tile_count)]
    owners, places = [], []
    for s in range(slots):
        row = home_ref[list_ref[0, s // length, s % length]]
        owner = row // shard_blocks
        rank = jnp.int32(0)
        for other in owners:
            rank = rank + jnp.where(other == owner, 1, 0)
        owners.append(owner)
        places.append(owner * capacity + rank)
        at_ref[s] = places[s]
        for o in range(tile_count):
            here = jnp.where(owner == o, row - owner * shard_blocks + 1, 0)
            asks[o] = asks[o] + jnp.where(lane == first + rank, here, 0)
    for o in range(tile_count):
        req[o] = asks[o]
    pl.semaphore_wait(barrier, len(others))
    for d in range(1, tile_count):
        give(*ask, d).start()

    for load in loads[2:]:
        load.wait()
    corr = corr_ref[...].astype(f4)
    opac = opac_ref[...].astype(f4)
    par[...] = jnp.zeros_like(par)
    for r in range(shard_blocks):
        par[r, 0:2, :] = centers_ref[r].astype(f4)
        par[r, 2:4, :] = scales_ref[r].astype(f4)
        par[r, 4:5, :] = corr[r:r + 1]
        par[r, 5:6, :] = opac[r:r + 1]
    wanted = req[me]
    for d in range(1, tile_count):
        given(*ask, d).wait_recv()
        wanted = wanted + req_in[sources[d]]
    table_v[...] = wanted
    move = local(table_v, table, table_sem)
    move.start()
    move.wait()

    def wanted_row(d, c):
        return jnp.maximum(table[0, peers[d] * capacity + c] - 1, 0)

    for d in range(1, tile_count):
        for c in range(capacity):
            par_out[peers[d], c] = par[wanted_row(d, c)].astype(bf)
        give(*pars, d).start()
    for d in range(1, tile_count):
        for c in range(capacity):
            feat_out[peers[d], c] = feat_ref[wanted_row(d, c)]
        give(*feats, d).start()
    for c in range(capacity):
        par_in[me, c] = par[wanted_row(0, c)].astype(bf)
        feat_in[me, c] = feat_ref[wanted_row(0, c)]

    kinds = lax.broadcasted_iota(jnp.int32, basis.shape, 0)
    basis[...] = basis_of(
        lax.broadcasted_iota(jnp.int32, basis.shape, 1), jnp.where(kinds < 24, kinds % 8, 7)
    )
    basis_t[...] = basis_of(
        lax.broadcasted_iota(jnp.int32, basis_t.shape, 0),
        lax.broadcasted_iota(jnp.int32, basis_t.shape, 1),
    )
    across = lax.broadcasted_iota(jnp.int32, lower.shape, 0)
    along = lax.broadcasted_iota(jnp.int32, lower.shape, 1)
    lower[...] = (along < across).astype(f4).astype(bf)
    upper[...] = (along > across).astype(f4).astype(bf)
    moment[...] = jnp.zeros_like(moment)
    dfeat[...] = jnp.zeros_like(dfeat)
    for q in range(tile_count * capacity):
        slot = jnp.int32(0)
        for s in range(slots):
            slot = slot + jnp.where(places[s] == q, s + 1, 0)
        slot_ref[q] = slot
    off_x = off_ref[0, 0]
    off_y = off_ref[0, 1]

    def entry(ref, s):
        q = at_ref[s]
        owner = q // capacity
        return ref[owner, q - owner * capacity]

    for d in range(1, tile_count):
        given(*pars, d).wait_recv()

    def prepare(s, carry):
        block = entry(par_in, s).astype(f4)
        prm[s] = block
        x, y, a, b, c, root = gaussian_terms(block, off_x, off_y)
        tile = s // length
        dead = s - tile * length >= length - pad_ref[0, tile]
        sig = jax.nn.log_sigmoid(block[5:6])
        const = sig - 0.5 * (a * x * x + 2.0 * b * x * y + c * y * y)
        const = jnp.where(dead, -10000.0, const)
        terms = jnp.concatenate(
            [const, a * x + b * y, b * x + c * y, -0.5 * a, -b, -0.5 * c,
             jnp.zeros((2, gauss), f4)], axis=0
        ) * LOG2E
        high = terms.astype(bf).astype(f4)
        rest = terms - high
        mid = rest.astype(bf).astype(f4)
        full = jnp.concatenate([high, mid, rest - mid, jnp.zeros((8, gauss), f4)], axis=0)
        coef[pl.ds(pl.multiple_of(s * gauss, gauss), gauss), :] = full.T.astype(bf)
        return carry

    lax.fori_loop(0, slots, prepare, 0)

    def forward(n, carry):
        tile = n // chunks
        start = pl.multiple_of((n - tile * chunks) * chunk, chunk)
        cot = cot_ref[0, tile, pl.ds(start, chunk), :]
        here = basis[:, pl.ds(start, chunk)]
        log_trans = jnp.zeros((1, chunk), f4)
        for p in range(pairs):
            base = pl.multiple_of(tile * (length * gauss) + p * span, span)
            at = (n, pl.ds(p * span, span))
            alpha = jnp.exp2(f32dot(coef[pl.ds(base, span), :], here))
            keep = 1.0 - alpha
            log_keep = jnp.log2(keep)
            high = log_keep.astype(bf)
            low = (log_keep - high.astype(f4)).astype(bf)
            before = f32dot(lower[...], high) + f32dot(lower[...], low) + log_trans
            w = alpha * jnp.exp2(before)
            log_trans = before[span - 1:span] + log_keep[span - 1:span]
            wb = w.astype(bf)
            weight[at] = wb
            exact[at] = w
            ratio[at] = alpha / keep
            slot = tile * length + p * PAIR
            more = f32dot(wb, cot)
            for i in range(PAIR):
                dfeat[slot + i] += more[i * gauss:(i + 1) * gauss]
        return carry

    lax.fori_loop(0, tiles * chunks, forward, 0)

    def outgoing(grad_ref, q):
        slot = slot_ref[q]
        return jnp.where(slot > 0, grad_ref[jnp.maximum(slot - 1, 0)], 0.0)

    for k in range(PIECES):
        for d in list(range(1, tile_count)) + [0]:
            for c in range(capacity):
                slot = slot_ref[peers[d] * capacity + c]
                got = dfeat[jnp.maximum(slot - 1, 0), k * piece:(k + 1) * piece, :]
                got = jnp.where(slot > 0, got, 0.0).astype(bf)
                if d:
                    grad_out[k, peers[d], c] = got
                else:
                    grad_in[k, me, c] = got
            if d:
                give(*grads[k], d).start()

    for d in range(1, tile_count):
        given(*feats, d).wait_recv()
    for s in range(slots):
        tile, place = s // length, s % length
        feature = entry(feat_in, s)
        blk[s] = feature
        feat_t[tile, :, place * gauss:(place + 1) * gauss] = transposed(feature)

    def backward(n, carry):
        tile = n // chunks
        start = pl.multiple_of((n - tile * chunks) * chunk, chunk)
        cot_t = transposed(cot_ref[0, tile, pl.ds(start, chunk), :])
        here_t = basis_t[pl.ds(start, chunk), :]
        later = jnp.zeros((1, chunk), f4)
        for p in reversed(range(pairs)):
            base = pl.multiple_of(tile * (length * gauss) + p * span, span)
            at = (n, pl.ds(p * span, span))
            slot = tile * length + p * PAIR
            feature = jnp.concatenate([blk[slot + i] for i in range(PAIR)], axis=0)
            gw = f32dot(feature, cot_t) * exact[at]
            after = f32dot(upper[...], gw.astype(bf)) + later
            later = after[0:1] + gw[0:1]
            slope = (gw - after * ratio[at]).astype(bf)
            moment[pl.ds(base, span), :] += f32dot(slope, here_t)
        image = f32dot(feat_t[tile], weight[n])
        image_ref[0, tile, pl.ds(start, chunk), :] = image.T.astype(bf)
        return carry

    def add_features(k):
        for d in range(1, tile_count):
            given(*grads[k], d).wait_recv()
        if total.shape[1] > shard_blocks * piece:
            total[k] = jnp.zeros(total.shape[1:], f4)

        def add(r, carry):
            acc = jnp.zeros((piece, width), f4)
            for t in range(tile_count):
                for c in range(capacity):
                    mark = jnp.where(table[0, t * capacity + c] == r + 1, 1.0, 0.0)
                    acc = acc + mark * grad_in[k, t, c].astype(f4)
            total[k, pl.ds(pl.multiple_of(r * piece, 16), piece), :] = acc
            return carry

        lax.fori_loop(0, shard_blocks, add, 0)

    def add_params():
        for d in range(1, tile_count):
            given(*dpars, d).wait_recv()
        total_p[...] = jnp.zeros_like(total_p)

        def add(r, carry):
            acc = jnp.zeros(dpar_in.shape[2:], f4)
            for t in range(tile_count):
                for c in range(capacity):
                    mark = jnp.where(table[0, t * capacity + c] == r + 1, 1.0, 0.0)
                    acc = acc + mark * dpar_in[t, c]
            total_p[pl.ds(pl.multiple_of(r * 8, 8), 8), :] = acc
            return carry

        lax.fori_loop(0, shard_blocks, add, 0)

    stage_count = 5

    def buffers_of(k):
        if k < PIECES:
            held = (total, pair_out, pair_in, chip_out, chip_in, done, out_ref)
            return tuple(ref.at[k] for ref in held)
        return total_p, pair_out_p, pair_in_p, chip_out_p, chip_in_p, done_p, out_par_ref

    def moves(k):
        _, p_out, p_in, c_out, c_in, fin, _ = buffers_of(k)

        def to_mate():
            return remote(p_out, p_in, pair_sem.at[k, 0], pair_sem.at[k, 1], mate)

        def to_chip(e):
            return remote(
                c_out.at[near[e]], c_in.at[chip], chip_send.at[k, e], chip_recv.at[k, chip],
                on_chip(near[e]),
            )

        def from_chip(e):
            c = behind[e]
            return remote(
                c_out.at[c], c_in.at[c], chip_send.at[k, e], chip_recv.at[k, c], on_chip(c)
            )

        def spread(e):
            return remote(
                fin.at[core, chip], fin.at[core, chip], done_send.at[k, e],
                done_recv.at[k, chip], on_chip(near[e]),
            )

        def spread_from(e):
            c = behind[e]
            return remote(
                fin.at[core, c], fin.at[core, c], done_send.at[k, e], done_recv.at[k, c],
                on_chip(c),
            )

        def pass_on(c):
            return remote(
                fin.at[core, c], fin.at[core, c], mate_send.at[k, c], mate_recv.at[k, c], mate
            )

        def passed(c):
            return remote(
                fin.at[1 - core, c], fin.at[1 - core, c], mate_send.at[k, c],
                mate_recv.at[k, c], mate,
            )

        return to_mate, to_chip, from_chip, spread, spread_from, pass_on, passed

    def advance(k, stage):
        tot, p_out, p_in, c_out, c_in, fin, out = buffers_of(k)
        to_mate, to_chip, from_chip, spread, spread_from, pass_on, passed = moves(k)
        part = fin.shape[2]

        def chunk_of(which, c):
            return pl.ds(pl.multiple_of((which * chips + c) * part, 16), part)

        if stage == 0:
            if k < PIECES:
                add_features(k)
            else:
                add_params()
            for c in range(chips):
                p_out[c] = tot[chunk_of(1 - core, c), :].astype(bf)
            to_mate().start()
        elif stage == 1:
            to_mate().wait_recv()
            for e in range(1, chips):
                c = near[e]
                c_out[c] = (tot[chunk_of(core, c), :] + p_in[c].astype(f4)).astype(bf)
                to_chip(e).start()
        elif stage == 2:
            mine = tot[chunk_of(core, chip), :] + p_in[chip].astype(f4)
            for e in range(1, chips):
                from_chip(e).wait_recv()
                mine = mine + c_in[behind[e]].astype(f4)
            fin[core, chip] = mine.astype(bf)
            for e in range(1, chips):
                spread(e).start()
            pass_on(chip).start()
        elif stage == 3:
            for e in range(1, chips):
                spread_from(e).wait_recv()
                pass_on(behind[e]).start()
        else:
            for e in range(chips):
                passed(behind[e]).wait_recv()
            for which in range(CORES):
                for c in range(chips):
                    out[which, c] = fin[which, c]

    def tick(t):
        for k in range(PIECES + 1):
            if 0 <= t - k < stage_count:
                advance(k, t - k)

    phases = PIECES if steps % PIECES == 0 else 1
    for phase in range(phases):
        each = steps // phases
        lax.fori_loop(phase * each, (phase + 1) * each, backward, 0)
        if 0 < phase:
            tick(phase - 1)

    def finish(s, carry):
        x, y, a, b, c, root = gaussian_terms(prm[s], off_x, off_y)
        m = moment[pl.ds(pl.multiple_of(s * gauss, gauss), gauss), :].T
        m0, m1, m2 = m[0:1], m[1:2], m[2:3]
        sx = m1 - x * m0
        sy = m2 - y * m0
        sxx = m[3:4] - 2.0 * x * m1 + x * x * m0
        sxy = m[4:5] - x * m2 - y * m1 + x * y * m0
        syy = m[5:6] - 2.0 * y * m2 + y * y * m0
        dpar[s] = jnp.concatenate(
            [a * sx + b * sy, b * sx + c * sy,
             -0.5 * (a * sxx + b * sxy), -0.5 * (c * syy + b * sxy),
             -root * sxy, jax.nn.sigmoid(-prm[s, 5:6, :]) * m0,
             jnp.zeros((2, gauss), f4)], axis=0
        )
        return carry

    lax.fori_loop(0, slots, finish, 0)
    for d in list(range(1, tile_count)) + [0]:
        for c in range(capacity):
            got = outgoing(dpar, peers[d] * capacity + c)
            if d:
                dpar_out[peers[d], c] = got
            else:
                dpar_in[me, c] = got
        if d:
            give(*dpars, d).start()

    for t in range(phases - 1, PIECES + stage_count):
        tick(t)
    for k in range(PIECES + 1):
        to_mate, to_chip, _, spread, _, pass_on, _ = moves(k)
        to_mate().wait_send()
        for e in range(1, chips):
            to_chip(e).wait_send()
            spread(e).wait_send()
        for e in range(chips):
            pass_on(behind[e]).wait_send()
    for d in range(1, tile_count):
        for buffers in [ask, pars, feats, dpars] + grads:
            give(*buffers, d).wait_send()


def splat(
    block_list, block_home, pads, offset, centers, log_scales, correlation, opacity_logit,
    features, cotangent, tile_count, views, capacity,
):
    _, tiles, pixels, width = cotangent.shape
    shard_blocks, gauss, _ = features.shape
    length = block_list.shape[2]
    slots = tiles * length
    spaces = tile_count * capacity
    chunk = 256
    steps = tiles * (pixels // chunk)
    total = slots * gauss
    piece = gauss // PIECES
    chips = views // CORES
    part = -(-shard_blocks * piece // (views * 16)) * 16
    part_p = -(-shard_blocks * 8 // (views * 16)) * 16
    bf, f4, i4 = jnp.bfloat16, jnp.float32, jnp.int32
    dma = pltpu.SemaphoreType.DMA
    each = dma((tile_count,))
    args = (
        block_list, block_home, pads, offset, centers, log_scales, correlation, opacity_logit,
        features, cotangent,
    )
    held = [pltpu.SMEM(a.shape, a.dtype) for a in args[:4]]
    held += [pltpu.VMEM(a.shape, a.dtype) for a in args[4:]]
    held += [dma((len(args),))]
    held += [
        pltpu.SMEM((slots,), i4), pltpu.SMEM((slots,), i4), pltpu.SMEM((spaces,), i4),
        pltpu.VMEM((tile_count, 8, 128), i4), pltpu.VMEM((tile_count, 8, 128), i4),
        pltpu.VMEM((8, 128), i4), pltpu.SMEM((8, 128), i4), dma, each, each,
        pltpu.VMEM((shard_blocks, ROWS, gauss), f4),
    ]
    held += [pltpu.VMEM((tile_count, capacity, ROWS, gauss), bf)] * 2
    held += [pltpu.VMEM((tile_count, capacity, gauss, width), bf)] * 2
    held += [each] * 4
    held += [
        pltpu.VMEM((slots, gauss, width), bf),
        pltpu.VMEM((slots, ROWS, gauss), f4),
        pltpu.VMEM((tiles, width, length * gauss), bf),
        pltpu.VMEM((total, 32), bf),
        pltpu.VMEM((32, pixels), bf),
        pltpu.VMEM((pixels, 128), bf),
        pltpu.VMEM((PAIR * gauss, PAIR * gauss), bf),
        pltpu.VMEM((PAIR * gauss, PAIR * gauss), bf),
        pltpu.VMEM((steps, length * gauss, chunk), bf),
        pltpu.VMEM((steps, length * gauss, chunk), f4),
        pltpu.VMEM((steps, length * gauss, chunk), f4),
        pltpu.VMEM((total, 128), f4),
        pltpu.VMEM((slots, gauss, width), f4),
        pltpu.VMEM((slots, 8, gauss), f4),
    ]
    held += [pltpu.VMEM((PIECES, tile_count, capacity, piece, width), bf)] * 2
    held += [pltpu.VMEM((tile_count, capacity, 8, gauss), f4)] * 2
    held += [dma((PIECES, tile_count))] * 2 + [each] * 2
    held += [pltpu.VMEM((PIECES, views * part, width), f4)]
    held += [pltpu.VMEM((PIECES, chips, part, width), bf)] * 4
    held += [pltpu.VMEM((PIECES, CORES, chips, part, width), bf)]
    held += [pltpu.VMEM((views * part_p, gauss), f4)]
    held += [pltpu.VMEM((chips, part_p, gauss), bf)] * 4
    held += [pltpu.VMEM((CORES, chips, part_p, gauss), bf)]
    held += [dma((PIECES + 1, 2))] + [dma((PIECES + 1, chips))] * 6
    return pl.pallas_call(
        functools.partial(splat_kernel, capacity, chunk),
        out_shape=(
            jax.ShapeDtypeStruct(cotangent.shape, bf),
            jax.ShapeDtypeStruct((PIECES, CORES, chips, part, width), bf),
            jax.ShapeDtypeStruct((CORES, chips, part_p, gauss), bf),
        ),
        in_specs=[ANY] * len(args),
        out_specs=(VMEM, VMEM, VMEM),
        scratch_shapes=held,
        compiler_params=pltpu.CompilerParams(
            collective_id=0, has_side_effects=True, vmem_limit_bytes=58 * 2**20
        ),
        name="splat",
    )(*args)


def unpack_kernel(
    image_hbm, sums_hbm, par_hbm,
    image_ref, centers_ref, scales_ref, corr_ref, opac_ref, feat_ref, sums, par, sem,
):
    shard_blocks, gauss, _ = feat_ref.shape
    pieces = sums.shape[0]
    piece = gauss // pieces
    move = local(image_hbm, image_ref, sem.at[0])
    move.start()
    loads = [local(par_hbm, par, sem.at[1])]
    loads += [local(sums_hbm.at[k], sums.at[k], sem.at[2 + k]) for k in range(pieces)]
    for load in loads:
        load.start()
    loads[0].wait()
    wide = par[...].astype(jnp.float32)
    for r in range(shard_blocks):
        row = wide[r * 8:(r + 1) * 8]
        centers_ref[r] = row[0:2]
        scales_ref[r] = row[2:4]
        corr_ref[r:r + 1, :] = row[4:5]
        opac_ref[r:r + 1, :] = row[5:6]
    for k in range(pieces):
        loads[1 + k].wait()
        for r in range(shard_blocks):
            feat_ref[r, k * piece:(k + 1) * piece, :] = (
                sums[k, r * piece:(r + 1) * piece, :].astype(jnp.float32)
            )
    move.wait()


def unpack(image, sums, par, shard_blocks, width, gauss):
    f4 = jnp.float32
    return pl.pallas_call(
        unpack_kernel,
        out_shape=(
            jax.ShapeDtypeStruct(image.shape, image.dtype),
            jax.ShapeDtypeStruct((shard_blocks, 2, gauss), f4),
            jax.ShapeDtypeStruct((shard_blocks, 2, gauss), f4),
            jax.ShapeDtypeStruct((shard_blocks, gauss), f4),
            jax.ShapeDtypeStruct((shard_blocks, gauss), f4),
            jax.ShapeDtypeStruct((shard_blocks, gauss, width), f4),
        ),
        in_specs=[ANY] * 3,
        out_specs=(ANY,) + (VMEM,) * 5,
        scratch_shapes=[
            pltpu.VMEM(sums.shape, sums.dtype),
            pltpu.VMEM(par.shape, par.dtype),
            pltpu.SemaphoreType.DMA((2 + sums.shape[0],)),
        ],
        compiler_params=pltpu.CompilerParams(vmem_limit_bytes=58 * 2**20),
        name="unpack",
    )(image, sums, par)


def shards(
    centers, log_scales, correlation, opacity_logit, features,
    view_offset, block_list, pad_count, block_home, image_grad,
):
    tile_count = lax.axis_size("tile")
    views = lax.axis_size("view")
    shard_blocks, gauss, width = features.shape
    slot_count = block_list.shape[1] * block_list.shape[2]
    capacity = (slot_count + tile_count - 1) // tile_count + 1
    image, sums, par = splat(
        block_list, block_home, pad_count, view_offset, centers, log_scales, correlation,
        opacity_logit, features, image_grad, tile_count, views, capacity,
    )
    sums = sums.reshape(sums.shape[0], -1, width)
    return tuple(unpack(image, sums, par.reshape(-1, gauss), shard_blocks, width, gauss))


def solution(mesh):
    in_specs = (
        P("tile", None, None),
        P("tile", None, None),
        P("tile", None),
        P("tile", None),
        P("tile", None, None),
        P("view", None),
        P("view", "tile", None),
        P("view", "tile"),
        P(),
        P("view", "tile", None, None),
    )
    out_specs = (
        P("view", "tile", None, None),
        P("tile", None, None),
        P("tile", None, None),
        P("tile", None),
        P("tile", None),
        P("tile", None, None),
    )
    return jax.shard_map(shards, mesh=mesh, in_specs=in_specs, out_specs=out_specs, check_vma=False)
```

```python
import functools

import jax
import jax.numpy as jnp
from jax import lax
from jax.experimental import pallas as pl
from jax.experimental.pallas import tpu as pltpu
from jax.sharding import PartitionSpec as P

TILE_W = 32
ROWS = 16
PAIR = 2
CORES = 2
PIECES = 2
LOG2E = 1.4426950408889634
SMEM = pl.BlockSpec(memory_space=pltpu.SMEM)
VMEM = pl.BlockSpec(memory_space=pltpu.VMEM)
ANY = pl.BlockSpec(memory_space=pl.ANY)
MESH = pl.DeviceIdType.MESH


def f32dot(a, b):
    return jnp.dot(a, b, preferred_element_type=jnp.float32)


def transposed(a):
    return a.astype(jnp.float32).T.astype(a.dtype)


def basis_of(pixel, kind):
    half = TILE_W // 2
    k = pixel % TILE_W - half
    j = pixel // TILE_W - half
    out = jnp.where(kind == 0, 1, 0)
    out = jnp.where(kind == 1, k, out)
    out = jnp.where(kind == 2, j, out)
    out = jnp.where(kind == 3, k * k, out)
    out = jnp.where(kind == 4, k * j, out)
    out = jnp.where(kind == 5, j * j, out)
    return out.astype(jnp.float32).astype(jnp.bfloat16)


def gaussian_terms(block, off_x, off_y):
    half = TILE_W // 2 + 0.0
    x = block[0:1] + (off_x - half - 0.5)
    y = block[1:2] + (off_y - half - 0.5)
    a = jnp.exp(block[2:3])
    c = jnp.exp(block[3:4])
    root = jnp.sqrt(a * c)
    b = block[4:5] * root
    return x, y, a, b, c, root


def remote(src, dst, send, recv, device):
    return pltpu.make_async_remote_copy(
        src_ref=src, dst_ref=dst, send_sem=send, recv_sem=recv,
        device_id=device, device_id_type=MESH,
    )


def local(src, dst, sem):
    return pltpu.make_async_copy(src, dst, sem)


def splat_kernel(
    capacity, chunk,
    list_hbm, home_hbm, pad_hbm, off_hbm, centers_hbm, scales_hbm, corr_hbm, opac_hbm,
    feat_hbm, cot_hbm,
    image_ref, out_ref, out_par_ref,
    list_ref, home_ref, pad_ref, off_ref, centers_ref, scales_ref, corr_ref, opac_ref,
    feat_ref, cot_ref, in_sem,
    at_ref, owner_ref, slot_ref, req, req_in, table_v, table, table_sem, req_send, req_recv,
    par, par_out, par_in, feat_out, feat_in,
    par_send, par_recv, feat_send, feat_recv,
    blk, prm, feat_t, coef, basis, basis_t, lower, upper,
    weight, exact, ratio, moment, dfeat, dpar,
    grad_out, grad_in, dpar_out, dpar_in, grad_send, grad_recv, dpar_send, dpar_recv,
    total, pair_out, pair_in, chip_out, chip_in, done,
    total_p, pair_out_p, pair_in_p, chip_out_p, chip_in_p, done_p,
    pair_sem, chip_send, chip_recv, done_send, done_recv, mate_send, mate_recv,
):
    _, tiles, length = list_ref.shape
    pixels = cot_ref.shape[2]
    slots = tiles * length
    shard_blocks, gauss, width = feat_ref.shape
    tile_count = req.shape[0]
    span = PAIR * gauss
    pairs = length // PAIR
    chunks = pixels // chunk
    steps = tiles * chunks
    chips = done.shape[2]
    piece = gauss // PIECES
    bf, f4 = jnp.bfloat16, jnp.float32

    me = lax.axis_index("tile")
    view = lax.axis_index("view")
    core = lax.rem(view, CORES)
    chip = view // CORES
    mate = {"view": chip * CORES + (1 - core)}
    peers = [lax.rem(me + d, tile_count) for d in range(tile_count)]
    sources = [lax.rem(me + tile_count - d, tile_count) for d in range(tile_count)]
    near = [lax.rem(chip + e, chips) for e in range(chips)]
    behind = [lax.rem(chip + chips - e, chips) for e in range(chips)]

    def on_chip(c):
        return {"view": c * CORES + core}

    def give(out, into, send, recv, d):
        return remote(out.at[peers[d]], into.at[me], send.at[d], recv.at[me], {"tile": peers[d]})

    def given(out, into, send, recv, d):
        s = sources[d]
        return remote(out.at[s], into.at[s], send.at[d], recv.at[s], {"tile": s})

    ask = (req, req_in, req_send, req_recv)
    pars = (par_out, par_in, par_send, par_recv)
    feats = (feat_out, feat_in, feat_send, feat_recv)
    grads = [
        tuple(ref.at[k] for ref in (grad_out, grad_in, grad_send, grad_recv))
        for k in range(PIECES)
    ]
    dpars = (dpar_out, dpar_in, dpar_send, dpar_recv)

    loads = [
        local(src, dst, in_sem.at[n]) for n, (src, dst) in enumerate((
            (list_hbm, list_ref), (home_hbm, home_ref), (pad_hbm, pad_ref), (off_hbm, off_ref),
            (centers_hbm, centers_ref), (scales_hbm, scales_ref), (corr_hbm, corr_ref),
            (opac_hbm, opac_ref), (feat_hbm, feat_ref), (cot_hbm, cot_ref),
        ))
    ]
    for load in loads:
        load.start()
    barrier = pltpu.get_barrier_semaphore()
    others = [{"tile": p} for p in peers[1:]] + [mate] + [on_chip(c) for c in near[1:]]
    for device in others:
        pl.semaphore_signal(barrier, inc=1, device_id=device, device_id_type=MESH)

    loads[0].wait()
    loads[1].wait()
    first = me * capacity
    lane = lax.broadcasted_iota(jnp.int32, req.shape[1:], 1)
    asks = [jnp.zeros(req.shape[1:], jnp.int32) for _ in range(tile_count)]
    owners, places = [], []
    for s in range(slots):
        row = home_ref[list_ref[0, s // length, s % length]]
        owner = row // shard_blocks
        rank = jnp.int32(0)
        for other in owners:
            rank = rank + jnp.where(other == owner, 1, 0)
        owners.append(owner)
        places.append(owner * capacity + rank)
        at_ref[s] = places[s]
        for o in range(tile_count):
            here = jnp.where(owner == o, row - owner * shard_blocks + 1, 0)
            asks[o] = asks[o] + jnp.where(lane == first + rank, here, 0)
    for o in range(tile_count):
        req[o] = asks[o]
    pl.semaphore_wait(barrier, len(others))
    for d in range(1, tile_count):
        give(*ask, d).start()

    for load in loads[2:]:
        load.wait()
    corr = corr_ref[...].astype(f4)
    opac = opac_ref[...].astype(f4)
    par[...] = jnp.zeros_like(par)
    for r in range(shard_blocks):
        par[r, 0:2, :] = centers_ref[r].astype(f4)
        par[r, 2:4, :] = scales_ref[r].astype(f4)
        par[r, 4:5, :] = corr[r:r + 1]
        par[r, 5:6, :] = opac[r:r + 1]
    wanted = req[me]
    for d in range(1, tile_count):
        given(*ask, d).wait_recv()
        wanted = wanted + req_in[sources[d]]
    table_v[...] = wanted
    move = local(table_v, table, table_sem)
    move.start()
    move.wait()

    def wanted_row(d, c):
        return jnp.maximum(table[0, peers[d] * capacity + c] - 1, 0)

    for d in range(1, tile_count):
        for c in range(capacity):
            par_out[peers[d], c] = par[wanted_row(d, c)].astype(bf)
        give(*pars, d).start()
    for d in range(1, tile_count):
        for c in range(capacity):
            feat_out[peers[d], c] = feat_ref[wanted_row(d, c)]
        give(*feats, d).start()
    for c in range(capacity):
        par_in[me, c] = par[wanted_row(0, c)].astype(bf)
        feat_in[me, c] = feat_ref[wanted_row(0, c)]

    kinds = lax.broadcasted_iota(jnp.int32, basis.shape, 0)
    basis[...] = basis_of(
        lax.broadcasted_iota(jnp.int32, basis.shape, 1), jnp.where(kinds < 24, kinds % 8, 7)
    )
    basis_t[...] = basis_of(
        lax.broadcasted_iota(jnp.int32, basis_t.shape, 0),
        lax.broadcasted_iota(jnp.int32, basis_t.shape, 1),
    )
    across = lax.broadcasted_iota(jnp.int32, lower.shape, 0)
    along = lax.broadcasted_iota(jnp.int32, lower.shape, 1)
    lower[...] = (along < across).astype(f4).astype(bf)
    upper[...] = (along > across).astype(f4).astype(bf)
    moment[...] = jnp.zeros_like(moment)
    dfeat[...] = jnp.zeros_like(dfeat)
    for q in range(tile_count * capacity):
        slot = jnp.int32(0)
        for s in range(slots):
            slot = slot + jnp.where(places[s] == q, s + 1, 0)
        slot_ref[q] = slot
    off_x = off_ref[0, 0]
    off_y = off_ref[0, 1]

    def entry(ref, s):
        q = at_ref[s]
        owner = q // capacity
        return ref[owner, q - owner * capacity]

    for d in range(1, tile_count):
        given(*pars, d).wait_recv()

    def prepare(s, carry):
        block = entry(par_in, s).astype(f4)
        prm[s] = block
        x, y, a, b, c, root = gaussian_terms(block, off_x, off_y)
        tile = s // length
        dead = s - tile * length >= length - pad_ref[0, tile]
        sig = jax.nn.log_sigmoid(block[5:6])
        const = sig - 0.5 * (a * x * x + 2.0 * b * x * y + c * y * y)
        const = jnp.where(dead, -10000.0, const)
        terms = jnp.concatenate(
            [const, a * x + b * y, b * x + c * y, -0.5 * a, -b, -0.5 * c,
             jnp.zeros((2, gauss), f4)], axis=0
        ) * LOG2E
        high = terms.astype(bf).astype(f4)
        rest = terms - high
        mid = rest.astype(bf).astype(f4)
        full = jnp.concatenate([high, mid, rest - mid, jnp.zeros((8, gauss), f4)], axis=0)
        coef[pl.ds(pl.multiple_of(s * gauss, gauss), gauss), :] = full.T.astype(bf)
        return carry

    lax.fori_loop(0, slots, prepare, 0)

    def forward(n, carry):
        tile = n // chunks
        start = pl.multiple_of((n - tile * chunks) * chunk, chunk)
        cot = cot_ref[0, tile, pl.ds(start, chunk), :]
        here = basis[:, pl.ds(start, chunk)]
        log_trans = jnp.zeros((1, chunk), f4)
        for p in range(pairs):
            base = pl.multiple_of(tile * (length * gauss) + p * span, span)
            at = (n, pl.ds(p * span, span))
            alpha = jnp.exp2(f32dot(coef[pl.ds(base, span), :], here))
            keep = 1.0 - alpha
            log_keep = jnp.log2(keep)
            high = log_keep.astype(bf)
            low = (log_keep - high.astype(f4)).astype(bf)
            before = f32dot(lower[...], high) + f32dot(lower[...], low) + log_trans
            w = alpha * jnp.exp2(before)
            log_trans = before[span - 1:span] + log_keep[span - 1:span]
            wb = w.astype(bf)
            weight[at] = wb
            exact[at] = w
            ratio[at] = alpha / keep
            slot = tile * length + p * PAIR
            more = f32dot(wb, cot)
            for i in range(PAIR):
                dfeat[slot + i] += more[i * gauss:(i + 1) * gauss]
        return carry

    lax.fori_loop(0, tiles * chunks, forward, 0)

    def outgoing(grad_ref, q):
        slot = slot_ref[q]
        return jnp.where(slot > 0, grad_ref[jnp.maximum(slot - 1, 0)], 0.0)

    for k in range(PIECES):
        for d in list(range(1, tile_count)) + [0]:
            for c in range(capacity):
                slot = slot_ref[peers[d] * capacity + c]
                got = dfeat[jnp.maximum(slot - 1, 0), k * piece:(k + 1) * piece, :]
                got = jnp.where(slot > 0, got, 0.0).astype(bf)
                if d:
                    grad_out[k, peers[d], c] = got
                else:
                    grad_in[k, me, c] = got
            if d:
                give(*grads[k], d).start()

    for d in range(1, tile_count):
        given(*feats, d).wait_recv()
    for s in range(slots):
        tile, place = s // length, s % length
        feature = entry(feat_in, s)
        blk[s] = feature
        feat_t[tile, :, place * gauss:(place + 1) * gauss] = transposed(feature)

    def backward(n, carry):
        tile = n // chunks
        start = pl.multiple_of((n - tile * chunks) * chunk, chunk)
        cot_t = transposed(cot_ref[0, tile, pl.ds(start, chunk), :])
        here_t = basis_t[pl.ds(start, chunk), :]
        later = jnp.zeros((1, chunk), f4)
        for p in reversed(range(pairs)):
            base = pl.multiple_of(tile * (length * gauss) + p * span, span)
            at = (n, pl.ds(p * span, span))
            slot = tile * length + p * PAIR
            feature = jnp.concatenate([blk[slot + i] for i in range(PAIR)], axis=0)
            gw = f32dot(feature, cot_t) * exact[at]
            after = f32dot(upper[...], gw.astype(bf)) + later
            later = after[0:1] + gw[0:1]
            slope = (gw - after * ratio[at]).astype(bf)
            moment[pl.ds(base, span), :] += f32dot(slope, here_t)
        image = f32dot(feat_t[tile], weight[n])
        image_ref[0, tile, pl.ds(start, chunk), :] = image.T.astype(bf)
        return carry

    def add_features(k):
        for d in range(1, tile_count):
            given(*grads[k], d).wait_recv()
        if total.shape[1] > shard_blocks * piece:
            total[k] = jnp.zeros(total.shape[1:], f4)

        def add(r, carry):
            acc = jnp.zeros((piece, width), f4)
            for t in range(tile_count):
                some = jnp.zeros((piece, width), bf)
                for c in range(capacity):
                    mark = jnp.where(table[0, t * capacity + c] == r + 1, 1.0, 0.0)
                    some = some + mark.astype(bf) * grad_in[k, t, c]
                acc = acc + some.astype(f4)
            total[k, pl.ds(pl.multiple_of(r * piece, 16), piece), :] = acc
            return carry

        lax.fori_loop(0, shard_blocks, add, 0)

    def add_params():
        for d in range(1, tile_count):
            given(*dpars, d).wait_recv()
        total_p[...] = jnp.zeros_like(total_p)

        def add(r, carry):
            acc = jnp.zeros(dpar_in.shape[2:], f4)
            for t in range(tile_count):
                for c in range(capacity):
                    mark = jnp.where(table[0, t * capacity + c] == r + 1, 1.0, 0.0)
                    acc = acc + mark * dpar_in[t, c]
            total_p[pl.ds(pl.multiple_of(r * 8, 8), 8), :] = acc
            return carry

        lax.fori_loop(0, shard_blocks, add, 0)

    stage_count = 5

    def buffers_of(k):
        if k < PIECES:
            held = (total, pair_out, pair_in, chip_out, chip_in, done, out_ref)
            return tuple(ref.at[k] for ref in held)
        return total_p, pair_out_p, pair_in_p, chip_out_p, chip_in_p, done_p, out_par_ref

    def moves(k):
        _, p_out, p_in, c_out, c_in, fin, _ = buffers_of(k)

        def to_mate():
            return remote(p_out, p_in, pair_sem.at[k, 0], pair_sem.at[k, 1], mate)

        def to_chip(e):
            return remote(
                c_out.at[near[e]], c_in.at[chip], chip_send.at[k, e], chip_recv.at[k, chip],
                on_chip(near[e]),
            )

        def from_chip(e):
            c = behind[e]
            return remote(
                c_out.at[c], c_in.at[c], chip_send.at[k, e], chip_recv.at[k, c], on_chip(c)
            )

        def spread(e):
            return remote(
                fin.at[core, chip], fin.at[core, chip], done_send.at[k, e],
                done_recv.at[k, chip], on_chip(near[e]),
            )

        def spread_from(e):
            c = behind[e]
            return remote(
                fin.at[core, c], fin.at[core, c], done_send.at[k, e], done_recv.at[k, c],
                on_chip(c),
            )

        def pass_on(c):
            return remote(
                fin.at[core, c], fin.at[core, c], mate_send.at[k, c], mate_recv.at[k, c], mate
            )

        def passed(c):
            return remote(
                fin.at[1 - core, c], fin.at[1 - core, c], mate_send.at[k, c],
                mate_recv.at[k, c], mate,
            )

        return to_mate, to_chip, from_chip, spread, spread_from, pass_on, passed

    def advance(k, stage):
        tot, p_out, p_in, c_out, c_in, fin, out = buffers_of(k)
        to_mate, to_chip, from_chip, spread, spread_from, pass_on, passed = moves(k)
        part = fin.shape[2]

        def chunk_of(which, c):
            return pl.ds(pl.multiple_of((which * chips + c) * part, 16), part)

        if stage == 0:
            if k < PIECES:
                add_features(k)
            else:
                add_params()
            for c in range(chips):
                p_out[c] = tot[chunk_of(1 - core, c), :].astype(bf)
            to_mate().start()
        elif stage == 1:
            to_mate().wait_recv()
            for e in range(1, chips):
                c = near[e]
                c_out[c] = (tot[chunk_of(core, c), :] + p_in[c].astype(f4)).astype(bf)
                to_chip(e).start()
        elif stage == 2:
            mine = tot[chunk_of(core, chip), :] + p_in[chip].astype(f4)
            for e in range(1, chips):
                from_chip(e).wait_recv()
                mine = mine + c_in[behind[e]].astype(f4)
            fin[core, chip] = mine.astype(bf)
            for e in range(1, chips):
                spread(e).start()
            pass_on(chip).start()
        elif stage == 3:
            for e in range(1, chips):
                spread_from(e).wait_recv()
                pass_on(behind[e]).start()
        else:
            for e in range(chips):
                passed(behind[e]).wait_recv()
            for which in range(CORES):
                for c in range(chips):
                    out[which, c] = fin[which, c]

    def tick(t):
        for k in range(PIECES + 1):
            if 0 <= t - k < stage_count:
                advance(k, t - k)

    lax.fori_loop(0, steps, backward, 0)

    def finish(s, carry):
        x, y, a, b, c, root = gaussian_terms(prm[s], off_x, off_y)
        m = moment[pl.ds(pl.multiple_of(s * gauss, gauss), gauss), :].T
        m0, m1, m2 = m[0:1], m[1:2], m[2:3]
        sx = m1 - x * m0
        sy = m2 - y * m0
        sxx = m[3:4] - 2.0 * x * m1 + x * x * m0
        sxy = m[4:5] - x * m2 - y * m1 + x * y * m0
        syy = m[5:6] - 2.0 * y * m2 + y * y * m0
        dpar[s] = jnp.concatenate(
            [a * sx + b * sy, b * sx + c * sy,
             -0.5 * (a * sxx + b * sxy), -0.5 * (c * syy + b * sxy),
             -root * sxy, jax.nn.sigmoid(-prm[s, 5:6, :]) * m0,
             jnp.zeros((2, gauss), f4)], axis=0
        )
        return carry

    lax.fori_loop(0, slots, finish, 0)
    for d in list(range(1, tile_count)) + [0]:
        for c in range(capacity):
            got = outgoing(dpar, peers[d] * capacity + c)
            if d:
                dpar_out[peers[d], c] = got
            else:
                dpar_in[me, c] = got
        if d:
            give(*dpars, d).start()

    for t in range(PIECES + stage_count):
        tick(t)
    for k in range(PIECES + 1):
        to_mate, to_chip, _, spread, _, pass_on, _ = moves(k)
        to_mate().wait_send()
        for e in range(1, chips):
            to_chip(e).wait_send()
            spread(e).wait_send()
        for e in range(chips):
            pass_on(behind[e]).wait_send()
    for d in range(1, tile_count):
        for buffers in [ask, pars, feats, dpars] + grads:
            give(*buffers, d).wait_send()


def splat(
    block_list, block_home, pads, offset, centers, log_scales, correlation, opacity_logit,
    features, cotangent, tile_count, views, capacity,
):
    _, tiles, pixels, width = cotangent.shape
    shard_blocks, gauss, _ = features.shape
    length = block_list.shape[2]
    slots = tiles * length
    spaces = tile_count * capacity
    chunk = 256
    steps = tiles * (pixels // chunk)
    total = slots * gauss
    piece = gauss // PIECES
    chips = views // CORES
    part = -(-shard_blocks * piece // (views * 16)) * 16
    part_p = -(-shard_blocks * 8 // (views * 16)) * 16
    bf, f4, i4 = jnp.bfloat16, jnp.float32, jnp.int32
    dma = pltpu.SemaphoreType.DMA
    each = dma((tile_count,))
    args = (
        block_list, block_home, pads, offset, centers, log_scales, correlation, opacity_logit,
        features, cotangent,
    )
    held = [pltpu.SMEM(a.shape, a.dtype) for a in args[:4]]
    held += [pltpu.VMEM(a.shape, a.dtype) for a in args[4:]]
    held += [dma((len(args),))]
    held += [
        pltpu.SMEM((slots,), i4), pltpu.SMEM((slots,), i4), pltpu.SMEM((spaces,), i4),
        pltpu.VMEM((tile_count, 8, 128), i4), pltpu.VMEM((tile_count, 8, 128), i4),
        pltpu.VMEM((8, 128), i4), pltpu.SMEM((8, 128), i4), dma, each, each,
        pltpu.VMEM((shard_blocks, ROWS, gauss), f4),
    ]
    held += [pltpu.VMEM((tile_count, capacity, ROWS, gauss), bf)] * 2
    held += [pltpu.VMEM((tile_count, capacity, gauss, width), bf)] * 2
    held += [each] * 4
    held += [
        pltpu.VMEM((slots, gauss, width), bf),
        pltpu.VMEM((slots, ROWS, gauss), f4),
        pltpu.VMEM((tiles, width, length * gauss), bf),
        pltpu.VMEM((total, 32), bf),
        pltpu.VMEM((32, pixels), bf),
        pltpu.VMEM((pixels, 128), bf),
        pltpu.VMEM((PAIR * gauss, PAIR * gauss), bf),
        pltpu.VMEM((PAIR * gauss, PAIR * gauss), bf),
        pltpu.VMEM((steps, length * gauss, chunk), bf),
        pltpu.VMEM((steps, length * gauss, chunk), f4),
        pltpu.VMEM((steps, length * gauss, chunk), f4),
        pltpu.VMEM((total, 128), f4),
        pltpu.VMEM((slots, gauss, width), f4),
        pltpu.VMEM((slots, 8, gauss), f4),
    ]
    held += [pltpu.VMEM((PIECES, tile_count, capacity, piece, width), bf)] * 2
    held += [pltpu.VMEM((tile_count, capacity, 8, gauss), f4)] * 2
    held += [dma((PIECES, tile_count))] * 2 + [each] * 2
    held += [pltpu.VMEM((PIECES, views * part, width), f4)]
    held += [pltpu.VMEM((PIECES, chips, part, width), bf)] * 4
    held += [pltpu.VMEM((PIECES, CORES, chips, part, width), bf)]
    held += [pltpu.VMEM((views * part_p, gauss), f4)]
    held += [pltpu.VMEM((chips, part_p, gauss), bf)] * 4
    held += [pltpu.VMEM((CORES, chips, part_p, gauss), bf)]
    held += [dma((PIECES + 1, 2))] + [dma((PIECES + 1, chips))] * 6
    return pl.pallas_call(
        functools.partial(splat_kernel, capacity, chunk),
        out_shape=(
            jax.ShapeDtypeStruct(cotangent.shape, bf),
            jax.ShapeDtypeStruct((PIECES, CORES, chips, part, width), bf),
            jax.ShapeDtypeStruct((CORES, chips, part_p, gauss), bf),
        ),
        in_specs=[ANY] * len(args),
        out_specs=(VMEM, VMEM, VMEM),
        scratch_shapes=held,
        compiler_params=pltpu.CompilerParams(
            collective_id=0, has_side_effects=True, vmem_limit_bytes=58 * 2**20
        ),
        name="splat",
    )(*args)


def unpack_kernel(
    image_hbm, sums_hbm, par_hbm,
    image_ref, centers_ref, scales_ref, corr_ref, opac_ref, feat_ref, held, sums, par, sem,
):
    shard_blocks, gauss, _ = feat_ref.shape
    pieces = sums.shape[0]
    piece = gauss // pieces
    bring = local(image_hbm, held, sem.at[0])
    bring.start()
    loads = [local(par_hbm, par, sem.at[1])]
    loads += [local(sums_hbm.at[k], sums.at[k], sem.at[2 + k]) for k in range(pieces)]
    for load in loads:
        load.start()
    bring.wait()
    move = local(held, image_ref, sem.at[0])
    move.start()
    loads[0].wait()
    wide = par[...].astype(jnp.float32)
    for r in range(shard_blocks):
        row = wide[r * 8:(r + 1) * 8]
        centers_ref[r] = row[0:2]
        scales_ref[r] = row[2:4]
        corr_ref[r:r + 1, :] = row[4:5]
        opac_ref[r:r + 1, :] = row[5:6]
    for k in range(pieces):
        loads[1 + k].wait()
        for r in range(shard_blocks):
            feat_ref[r, k * piece:(k + 1) * piece, :] = (
                sums[k, r * piece:(r + 1) * piece, :].astype(jnp.float32)
            )
    move.wait()


def unpack(image, sums, par, shard_blocks, width, gauss):
    f4 = jnp.float32
    return pl.pallas_call(
        unpack_kernel,
        out_shape=(
            jax.ShapeDtypeStruct(image.shape, image.dtype),
            jax.ShapeDtypeStruct((shard_blocks, 2, gauss), f4),
            jax.ShapeDtypeStruct((shard_blocks, 2, gauss), f4),
            jax.ShapeDtypeStruct((shard_blocks, gauss), f4),
            jax.ShapeDtypeStruct((shard_blocks, gauss), f4),
            jax.ShapeDtypeStruct((shard_blocks, gauss, width), f4),
        ),
        in_specs=[ANY] * 3,
        out_specs=(ANY,) + (VMEM,) * 5,
        scratch_shapes=[
            pltpu.VMEM(image.shape, image.dtype),
            pltpu.VMEM(sums.shape, sums.dtype),
            pltpu.VMEM(par.shape, par.dtype),
            pltpu.SemaphoreType.DMA((2 + sums.shape[0],)),
        ],
        compiler_params=pltpu.CompilerParams(vmem_limit_bytes=58 * 2**20),
        name="unpack",
    )(image, sums, par)


def shards(
    centers, log_scales, correlation, opacity_logit, features,
    view_offset, block_list, pad_count, block_home, image_grad,
):
    tile_count = lax.axis_size("tile")
    views = lax.axis_size("view")
    shard_blocks, gauss, width = features.shape
    slot_count = block_list.shape[1] * block_list.shape[2]
    capacity = (slot_count + tile_count - 1) // tile_count + 1
    image, sums, par = splat(
        block_list, block_home, pad_count, view_offset, centers, log_scales, correlation,
        opacity_logit, features, image_grad, tile_count, views, capacity,
    )
    sums = sums.reshape(sums.shape[0], -1, width)
    return tuple(unpack(image, sums, par.reshape(-1, gauss), shard_blocks, width, gauss))


def solution(mesh):
    in_specs = (
        P("tile", None, None),
        P("tile", None, None),
        P("tile", None),
        P("tile", None),
        P("tile", None, None),
        P("view", None),
        P("view", "tile", None),
        P("view", "tile"),
        P(),
        P("view", "tile", None, None),
    )
    out_specs = (
        P("view", "tile", None, None),
        P("tile", None, None),
        P("tile", None, None),
        P("tile", None),
        P("tile", None),
        P("tile", None, None),
    )
    return jax.shard_map(shards, mesh=mesh, in_specs=in_specs, out_specs=out_specs, check_vma=False)
```
